32 devices in a mesh: row: 4 (over z), col: 8 (over y, x, core).
Axes of the slice: x: 2, y: 2, z: 4, core: 2. Of those that a mesh axis runs over, the one named last changes fastest.
Arguments:
- ancestor_inverse: bfloat16 [6144, 6144], P('row', 'col'), may hold values from -6 to 6
- factor_slots: bfloat16 [3, 4096, 512], P(None, ('row', 'col')), may hold values from -0.25 to 0.25
- slot_tiles: int32 [3, 16], replicated, may hold values from -1 to 23, as said below
- parent_factor: bfloat16 [2, 512, 512], replicated, may hold values from -0.25 to 0.25
- diag_inverse: float32 [3, 512, 512], replicated, may hold values from -6 to 6
Outputs:
- inverse_panels: bfloat16 [3, 6144, 512], P(None, ('row', 'col'))
- diag_blocks: float32 [3, 512, 512], replicated
- parent_blocks: float32 [2, 512, 512], replicated
The draws below stay inside these ranges and needn't reach their ends.
Inputs may be any that keep to these rules, and one draw needn't show every extreme that they name: `slot_tiles`: entries b * 2 to b * 2 + 1 of a supernode's row are the slots of column block b: each is -1 (empty) or names a tile from b * 3 to b * 3 + 2, no tile twice; in each supernode some block has all its slots filled. `factor_slots`: rows of an empty slot are not part of the factor.
All inputs are finite; a program needn't handle non-finite values.
Results may differ from the reference program's by a relative error of at most 0.00075.
Values may be sent and summed in bfloat16 or wider, within the bound.
A program may use at most 128 MiB of HBM per device.

```python
import jax
import jax.numpy as jnp
from jax import lax

TILE = 256
W = 512
TPC = 3
CAP = 2
NODES = 3
BLOCKS = 8
NA = 6144
SLOTS = 16


def draw_slot_tiles(key, part):
    base = jax.random.fold_in(key, 17)
    count_key, forced_key, score_key = jax.random.split(base, 3)
    counts = jax.random.randint(count_key, (NODES, BLOCKS), 0, CAP + 1)
    forced = jax.random.randint(forced_key, (NODES,), 0, BLOCKS)
    counts = jnp.where(jnp.arange(BLOCKS)[None, :] == forced[:, None], CAP, counts)
    scores = jax.random.randint(score_key, (NODES, BLOCKS, TPC), 0, 1 << 20)
    scores = scores * TPC + jnp.arange(TPC)[None, None, :]
    ranking = jnp.argsort(scores, axis=-1)[:, :, :CAP]
    tiles = jnp.arange(BLOCKS)[None, :, None] * TPC + ranking
    filled = jnp.arange(CAP)[None, None, :] < counts[:, :, None]
    result = jnp.where(filled, tiles, -1)
    return result.reshape(NODES, BLOCKS * CAP).astype(jnp.int32)


def raised(drawn, stream_key, source, target, shards_of, factor):
    owner, partner = [(jnp.arange(drawn.shape[axis_at]) // (drawn.shape[axis_at] // shards_of)).reshape([-1 if axis == axis_at else 1 for axis in range(drawn.ndim)]) for axis_at in (source, target)]
    chosen = jax.random.permutation(stream_key, shards_of)[partner]
    strong = (owner == chosen) | (owner == (partner + shards_of // 2) % shards_of)
    return jnp.where(strong, factor * drawn, drawn)


def level_of(stream_key, shape, cuts, smallest, largest):
    def one(position, blocks):
        heights = jax.random.uniform(jax.random.fold_in(jax.random.fold_in(stream_key, 6), position), (blocks,), jnp.float32, smallest / len(cuts), largest / len(cuts))
        return jnp.repeat(jnp.exp(heights), shape[position] // blocks).reshape((-1,) + (1,) * (len(shape) - position - 1))

    loudness = one(*cuts[0])
    for cut in cuts[1:]:
        loudness = loudness * one(*cut)
    return loudness


def noise(key, extent, deviation, most, cuts=(), kind=jnp.bfloat16):
    values = deviation * jax.random.normal(key, extent, jnp.float32)
    if cuts:
        values = values * level_of(key, extent, cuts, -0.22, 0.18)
    return jnp.clip(values, -most, most).astype(kind)


def bell_draw_with(own_key, shape, deviation, limit, cuts, heavy, held_as=jnp.bfloat16):
    values = deviation * jax.random.normal(own_key, shape, jnp.float32)
    if cuts:
        values = values * level_of(own_key, shape, cuts, -0.22, 0.18)
    return jnp.clip(raised(values, jax.random.fold_in(own_key, 3), *heavy), -limit, limit).astype(held_as)


def setup_inputs(seed: int = 0) -> dict:
    splits = jax.random.split(jax.random.key(seed), 6)
    return {
        "ancestor_inverse": noise(splits[0], (NA, NA), 1.0, 6.0, ((0, 4), (1, 8))),
        "factor_slots": bell_draw_with(splits[1], (NODES, SLOTS * TILE, W), (NA // 3) ** -0.5, 0.25, ((1, 32),), (1, 2, 32, 2.75)),
        "slot_tiles": draw_slot_tiles(jax.random.fold_in(splits[5], 71), 0),
        "parent_factor": noise(splits[3], (NODES - 1, W, W), W ** -0.5, 0.25),
        "diag_inverse": noise(splits[4], (NODES, W, W), 1.0, 6.0, (), jnp.float32),
    }


exact_mode = lax.Precision.HIGHEST


def block_panel(ancestor_inverse, factor_node, tiles_node, block_index):
    slot_ids = lax.dynamic_slice_in_dim(tiles_node, block_index * CAP, CAP)
    slot_data = lax.dynamic_slice_in_dim(factor_node, block_index * CAP * TILE, CAP * TILE, 0)
    columns = lax.dynamic_slice_in_dim(ancestor_inverse, block_index * TPC * TILE, TPC * TILE, 1)
    local_tile = slot_ids - block_index * TPC
    pieces = []
    for tile_index in range(TPC):
        chosen = jnp.zeros((TILE, W), jnp.bfloat16)
        for member in range(CAP):
            chosen = jnp.where(local_tile[member] == tile_index, slot_data[member * TILE:(member + 1) * TILE], chosen)
        pieces.append(chosen)
    padded = jnp.concatenate(pieces, axis=0)
    product = jnp.dot(columns, padded, preferred_element_type=jnp.float32)
    return product, padded


def node_panel(ancestor_inverse, factor_node, tiles_node):
    def one_block(total, block_index):
        product, padded = block_panel(ancestor_inverse, factor_node, tiles_node, block_index)
        return total + product, padded

    start_total = jnp.zeros((NA, W), jnp.float32)
    total, padded_all = lax.scan(one_block, start_total, jnp.arange(BLOCKS, dtype=jnp.int32))
    return total, padded_all.reshape(NA, W)


def reference(ancestor_inverse, factor_slots, slot_tiles, parent_factor, diag_inverse):
    panels = []
    diagonals = []
    parents = []
    previous = None
    prev_diag = None
    for node in range(NODES):
        total, padded = node_panel(ancestor_inverse, factor_slots[node], slot_tiles[node])
        dense = padded.astype(jnp.float32)
        column = -total
        if node > 0:
            parent_link = parent_factor[node - 1].astype(jnp.float32)
            column = column - jnp.dot(previous, parent_link, precision=exact_mode)
        first_term = jnp.dot(dense.T, column, precision=exact_mode)
        if node > 0:
            second_term = jnp.dot(previous.T, dense, precision=exact_mode)
            upper = -(second_term + jnp.dot(prev_diag, parent_link, precision=exact_mode))
            diagonal = diag_inverse[node] - first_term - jnp.dot(parent_link.T, upper, precision=exact_mode)
            parents.append(upper)
        else:
            diagonal = diag_inverse[0] - first_term
        panels.append(column.astype(jnp.bfloat16))
        diagonals.append(diagonal)
        previous = column
        prev_diag = diagonal
    return jnp.stack(panels), jnp.stack(diagonals), jnp.stack(parents)
```

```python
import functools

import jax
import jax.numpy as jnp
from jax import lax
from jax.experimental import pallas as pl
from jax.experimental.pallas import tpu as pltpu
from jax.sharding import PartitionSpec as P

TILE = 256
CAP = 2


exact_mode = lax.Precision.HIGHEST


VMEM = pl.BlockSpec(memory_space=pltpu.VMEM)


def send(src, dst, send_sem, recv_sem, row, col):
    copy = pltpu.make_async_remote_copy(
        src_ref=src,
        dst_ref=dst,
        send_sem=send_sem,
        recv_sem=recv_sem,
        device_id=(row, col),
        device_id_type=pl.DeviceIdType.MESH,
    )
    copy.start()
    return copy


def greet(peers):
    barrier = pltpu.get_barrier_semaphore()
    for row, col in peers:
        pl.semaphore_signal(
            barrier, inc=1, device_id=(row, col), device_id_type=pl.DeviceIdType.MESH
        )
    pl.semaphore_wait(barrier, len(peers))


def distribute_kernel(
    row_count, col_count, piece, weights, own, passed,
    z_send, z_recv, w_send, w_recv, own_send, own_recv, local_sem,
):
    row, col = lax.axis_index("row"), lax.axis_index("col")
    groups = col_count // row_count
    rows = piece.shape[1]
    place, group = lax.rem(col, row_count), lax.div(col, row_count)
    greet(
        [(lax.rem(row + step, row_count), col) for step in range(1, row_count)]
        + [(row, lax.rem(col + step, col_count)) for step in range(1, col_count)]
    )
    here = pl.ds(pl.multiple_of(place * rows, rows), rows)

    copies = []
    for step in range(1, row_count):
        copies.append(
            send(
                piece, passed.at[step - 1], z_send.at[step - 1], z_recv.at[step - 1],
                lax.rem(row + step, row_count), col,
            )
        )

    def deliver(step, source):
        target = lax.rem(row - step + row_count, row_count) * groups + group

        def make():
            return pltpu.make_async_remote_copy(
                src_ref=source,
                dst_ref=weights.at[:, here, :],
                send_sem=w_send.at[step],
                recv_sem=w_recv.at[place],
                device_id=(row, target),
                device_id_type=pl.DeviceIdType.MESH,
            )

        @pl.when(target != col)
        def _():
            make().start()

        @pl.when(target == col)
        def _():
            pltpu.make_async_copy(source, weights.at[:, here, :], w_send.at[step]).start()

        return step, target, make, source

    delivered = [deliver(0, piece)]
    local = pltpu.make_async_copy(piece, own.at[:, here, :], local_sem)
    local.start()
    own_copies = []
    for step in range(1, row_count):
        own_copies.append(
            send(
                piece, own.at[:, here, :], own_send.at[step - 1], own_recv.at[step - 1],
                row, group * row_count + lax.rem(place + step, row_count),
            )
        )
    for step in range(1, row_count):
        copies[step - 1].wait_recv()
        delivered.append(deliver(step, passed.at[step - 1]))
    for step, target, make, source in delivered:

        @pl.when(target != col)
        def _():
            make().wait_send()

        @pl.when(target == col)
        def _():
            pltpu.make_async_copy(source, weights.at[:, here, :], w_send.at[step]).wait()

    for slot in range(row_count):
        origin = lax.rem(col, groups) * row_count + slot

        @pl.when(origin != col)
        def _():
            pltpu.make_async_remote_copy(
                src_ref=piece,
                dst_ref=weights.at[:, pl.ds(slot * rows, rows), :],
                send_sem=w_send.at[0],
                recv_sem=w_recv.at[slot],
                device_id=(row, origin),
                device_id_type=pl.DeviceIdType.MESH,
            ).wait_recv()

    local.wait()
    for copy in copies:
        copy.wait_send()
    for step in range(1, row_count):
        own_copies[step - 1].wait_send()
        from_place = lax.rem(place - step + row_count, row_count)
        pltpu.make_async_remote_copy(
            src_ref=piece,
            dst_ref=own.at[:, pl.ds(pl.multiple_of(from_place * rows, rows), rows), :],
            send_sem=own_send.at[step - 1],
            recv_sem=own_recv.at[step - 1],
            device_id=(row, group * row_count + from_place),
            device_id_type=pl.DeviceIdType.MESH,
        ).wait_recv()


def distribute(factor_slots, row_count, col_count):
    nodes, rows, width = factor_slots.shape
    gathered = jax.ShapeDtypeStruct((nodes, row_count * rows, width), factor_slots.dtype)
    dma = pltpu.SemaphoreType.DMA
    return pl.pallas_call(
        functools.partial(distribute_kernel, row_count, col_count),
        out_shape=(gathered, gathered),
        in_specs=[VMEM],
        out_specs=(VMEM, VMEM),
        scratch_shapes=[
            pltpu.VMEM((row_count - 1, nodes, rows, width), factor_slots.dtype),
            dma((row_count - 1,)),
            dma((row_count - 1,)),
            dma((row_count,)),
            dma((row_count,)),
            dma((row_count - 1,)),
            dma((row_count - 1,)),
            dma,
        ],
        compiler_params=pltpu.CompilerParams(
            collective_id=0, has_side_effects=True, vmem_limit_bytes=40 * 2**20
        ),
        name="distribute",
    )(factor_slots)


def bits_of(count):
    return [1 << place for place in range(count.bit_length() - 1)]


def sum_kernel(orders, bounds, given, out, total, landed, rs_send, rs_recv, ag_send, ag_recv):
    index = {"row": lax.axis_index("row"), "col": lax.axis_index("col")}

    def partner(bit):
        axis, weight = bit
        mine = lax.rem(lax.div(index[axis], weight), 2)
        moved = dict(index)
        moved[axis] = index[axis] + (1 - 2 * mine) * weight
        return mine, moved["row"], moved["col"]

    greet([partner(bit)[1:] for bit in sorted(orders[0])])
    steps = len(orders[0])
    starts = [[base] for base, _ in bounds]
    copies = {}
    landing = [base for base, _ in bounds]

    def rows_at(start, length):
        return pl.ds(pl.multiple_of(start, 8), length)

    def halve(part, step):
        half = bounds[part][1] >> (step + 1)
        mine, row, col = partner(orders[part][step])
        start = starts[part][step]
        source = given if step == 0 else total
        copies[part, step] = send(
            source.at[rows_at(start + (1 - mine) * half, half)],
            landed.at[pl.ds(landing[part], half)],
            rs_send.at[part, step], rs_recv.at[part, step], row, col,
        )
        starts[part].append(start + mine * half)

    def add(part, step):
        half = bounds[part][1] >> (step + 1)
        start = starts[part][step + 1]
        source = given if step == 0 else total
        target = out if step == steps - 1 else total
        chunk = min(half, 32)

        def body(turn, carry):
            rows = rows_at(start + turn * chunk, chunk)
            target[rows, :] = (
                source[rows, :] + landed[rows_at(landing[part] + turn * chunk, chunk), :]
            )
            return carry

        lax.fori_loop(0, half // chunk, body, 0)
        landing[part] += half

    def double(part, step):
        length = bounds[part][1] >> (step + 1)
        _, row, col = partner(orders[part][step])
        where = rows_at(starts[part][step + 1], length)
        copies[part, steps + step] = send(
            out.at[where], out.at[where], ag_send.at[part, step], ag_recv.at[part, step], row, col
        )

    parts = range(len(orders))
    for part in parts:
        halve(part, 0)
    for step in range(steps):
        for part in parts:
            copies[part, step].wait_recv()
            add(part, step)
            if step + 1 < steps:
                halve(part, step + 1)
            else:
                double(part, step)
    for step in range(steps - 1, -1, -1):
        for part in parts:
            half = bounds[part][1] >> (step + 1)
            mine, row, col = partner(orders[part][step])
            pltpu.make_async_remote_copy(
                src_ref=out.at[rows_at(starts[part][step + 1], half)],
                dst_ref=out.at[rows_at(starts[part][step] + (1 - mine) * half, half)],
                send_sem=ag_send.at[part, step],
                recv_sem=ag_recv.at[part, step],
                device_id=(row, col),
                device_id_type=pl.DeviceIdType.MESH,
            ).wait_recv()
            if step > 0:
                double(part, step - 1)
    for copy in copies.values():
        copy.wait_send()


def sum_all(given, row_count, col_count):
    rows, width = given.shape
    col_bits, row_bits = bits_of(col_count), bits_of(row_count)
    half = 1 + (len(col_bits) - 1) // 2
    core = [("col", bit) for bit in col_bits[:1]]
    x = [("col", bit) for bit in col_bits[1:half]]
    y = [("col", bit) for bit in col_bits[half:]]
    z = [("row", bit) for bit in row_bits]
    orders = (core + x + y + z, core + y + x + z, core + z + x + y)
    unit = 8 * row_count * col_count
    units = max(3, -(-rows // unit))
    shares = (-(-units * 2 // 5), -(-units * 2 // 5))
    if units < 5:
        shares = (1, 1)
    shares = shares + (units - sum(shares),)
    bounds, base = [], 0
    for share in shares:
        bounds.append((base, share * unit))
        base += share * unit
    if base > rows:
        given = jnp.concatenate([given, jnp.zeros((base - rows, width), given.dtype)])
    shape = (base, width)
    dma = pltpu.SemaphoreType.DMA((len(orders), len(orders[0])))
    out = pl.pallas_call(
        functools.partial(sum_kernel, orders, bounds),
        out_shape=jax.ShapeDtypeStruct(shape, given.dtype),
        in_specs=[VMEM],
        out_specs=VMEM,
        scratch_shapes=[
            pltpu.VMEM(shape, given.dtype),
            pltpu.VMEM(shape, given.dtype),
            dma, dma, dma, dma,
        ],
        compiler_params=pltpu.CompilerParams(
            collective_id=1, has_side_effects=True, vmem_limit_bytes=56 * 2**20
        ),
        name="sum_all",
    )(given)
    return out[:rows]


def padded_block(slot_data, slot_ids, block_index, tiles_per_block, tile_rows):
    local_tile = slot_ids - block_index * tiles_per_block
    pieces = []
    for tile_index in range(tiles_per_block):
        chosen = jnp.zeros((tile_rows, slot_data.shape[1]), slot_data.dtype)
        for member in range(slot_ids.shape[0]):
            chosen = jnp.where(
                local_tile[member] == tile_index,
                slot_data[member * tile_rows : (member + 1) * tile_rows],
                chosen,
            )
        pieces.append(chosen)
    return jnp.concatenate(pieces, axis=0)


def chosen_columns(inverse_block, slot_ids, block_index, tiles_per_block, tile_rows):
    local_tile = jnp.clip(slot_ids - block_index * tiles_per_block, 0, tiles_per_block - 1)
    pieces = [
        lax.dynamic_slice_in_dim(inverse_block, local_tile[member] * tile_rows, tile_rows, 1)
        for member in range(slot_ids.shape[0])
    ]
    return jnp.concatenate(pieces, axis=1)


def masked_rows(slot_data, slot_ids, tile_rows):
    live_rows = jnp.repeat(slot_ids >= 0, tile_rows)
    return jnp.where(live_rows[:, None], slot_data, jnp.zeros_like(slot_data))


def on_device(ancestor_inverse, factor_slots, slot_tiles, parent_factor, diag_inverse):
    row_count = lax.axis_size("row")
    col_count = lax.axis_size("col")
    row_index = lax.axis_index("row")
    col_index = lax.axis_index("col")
    block_rows, block_cols = ancestor_inverse.shape
    tile_rows = TILE
    tiles_per_block = block_cols // tile_rows
    node_count = factor_slots.shape[0]
    panel_width = factor_slots.shape[2]
    slot_count = CAP
    slot_rows = slot_count * tile_rows
    groups_per_row = col_count // row_count
    panel_rows = block_rows // col_count
    own_block = row_index * groups_per_row + col_index // row_count
    own_offset = col_index % row_count * panel_rows

    def prepare(node, own_slots, col_slots):
        tiles_node = slot_tiles[node]
        col_ids = lax.dynamic_slice_in_dim(tiles_node, col_index * slot_count, slot_count)
        columns = chosen_columns(ancestor_inverse, col_ids, col_index, tiles_per_block, tile_rows)
        weights = masked_rows(col_slots, col_ids, tile_rows)
        own_ids = lax.dynamic_slice_in_dim(tiles_node, own_block * slot_count, slot_count)
        own_padded = padded_block(own_slots, own_ids, own_block, tiles_per_block, tile_rows)
        own_rows = lax.dynamic_slice_in_dim(own_padded, own_offset, panel_rows, 0)
        return (columns, weights, own_rows.astype(jnp.float32))

    def finish(node, first_total, second_total, prev_diag):
        if node == 0:
            return (diag_inverse[0] - first_total, None)
        parent_link = parent_factor[node - 1].astype(jnp.float32)
        upper = -(second_total + jnp.dot(prev_diag, parent_link, precision=exact_mode))
        diagonal = (
            diag_inverse[node] - first_total - jnp.dot(parent_link.T, upper, precision=exact_mode)
        )
        return (diagonal, upper)

    panels = []
    diagonals = []
    parents = []
    col_all, own_all = distribute(factor_slots, row_count, col_count)
    prepared = [prepare(node, own_all[node], col_all[node]) for node in range(node_count)]
    firsts = []
    summed_all = lax.psum_scatter(
        jnp.concatenate(
            [jnp.dot(entry[0], entry[1], preferred_element_type=jnp.float32) for entry in prepared],
            axis=1,
        ),
        "col",
        scatter_dimension=0,
        tiled=True,
    )
    previous = None
    seconds = []
    for node in range(node_count):
        own_rows = prepared[node][2]
        summed = summed_all[:, node * panel_width : (node + 1) * panel_width]
        column = -summed
        if node > 0:
            advance_parent_link = parent_factor[node - 1].astype(jnp.float32)
            column = column - jnp.dot(previous, advance_parent_link, precision=exact_mode)
        if node > 0:
            seconds.append(jnp.dot(previous.T, own_rows, precision=exact_mode))
        firsts.append(jnp.dot(own_rows.T, column, precision=exact_mode))
        panels.append(column.astype(jnp.bfloat16))
        previous = column
    totals = sum_all(jnp.concatenate(firsts + seconds, axis=0), row_count, col_count)
    totals = totals.reshape(-1, panel_width, panel_width)
    first_totals, second_totals = totals[:node_count], totals[node_count:]
    prev_diag = None
    for node in range(node_count):
        second_total = second_totals[node - 1] if node > 0 else None
        diagonal, upper = finish(node, first_totals[node], second_total, prev_diag)
        diagonals.append(diagonal)
        if node > 0:
            parents.append(upper)
        prev_diag = diagonal
    return (jnp.stack(panels), jnp.stack(diagonals), jnp.stack(parents))


def solution(mesh):
    placed = (P("row", "col"), P(None, ("row", "col"), None), P(), P(), P())
    return jax.shard_map(
        on_device,
        mesh=mesh,
        in_specs=placed,
        out_specs=(P(None, ("row", "col"), None), P(), P()),
        check_vma=False,
    )
```

```python
import functools

import jax
import jax.numpy as jnp
from jax import lax
from jax.experimental import pallas as pl
from jax.experimental.pallas import tpu as pltpu
from jax.sharding import PartitionSpec as P

TILE = 256
CAP = 2


exact_mode = lax.Precision.HIGHEST


VMEM = pl.BlockSpec(memory_space=pltpu.VMEM)


def send(src, dst, send_sem, recv_sem, row, col):
    copy = pltpu.make_async_remote_copy(
        src_ref=src,
        dst_ref=dst,
        send_sem=send_sem,
        recv_sem=recv_sem,
        device_id=(row, col),
        device_id_type=pl.DeviceIdType.MESH,
    )
    copy.start()
    return copy


def greet(peers):
    barrier = pltpu.get_barrier_semaphore()
    for row, col in peers:
        pl.semaphore_signal(
            barrier, inc=1, device_id=(row, col), device_id_type=pl.DeviceIdType.MESH
        )
    pl.semaphore_wait(barrier, len(peers))


def bits_of(count):
    return [1 << place for place in range(count.bit_length() - 1)]


def flipped(place, mask, bits):
    for bit in bits:
        if mask & bit:
            place = place + (1 - 2 * lax.rem(lax.div(place, bit), 2)) * bit
    return place


def panels_kernel(
    row_count, col_count, chosen, ancestor, piece, summed, own, *scratch
):
    (weights, dense, passed, given_core, core_in, z_send, z_recv, w_send, w_recv, own_send, own_recv,
     local_sem, core_send, core_recv, rs_send, rs_recv) = scratch[:16]
    levels = bits_of(col_count)[1:]
    held = [scratch[16:16 + len(levels)], scratch[16 + len(levels):16 + 2 * len(levels)]]
    rest = scratch[16 + 2 * len(levels):]
    came = [rest[:len(levels)], rest[len(levels):]]
    orders = [levels, levels[::-1]]
    row, col = lax.axis_index("row"), lax.axis_index("col")
    groups = col_count // row_count
    nodes, rows, width = piece.shape
    half_width = width // 2
    place, group = lax.rem(col, row_count), lax.div(col, row_count)
    core = lax.rem(col, 2)
    mates, panel_rows = ancestor.shape[0], ancestor.shape[2]
    slot_rows = TILE
    tiles_per_block = ancestor.shape[3] // slot_rows
    greet(
        [(lax.rem(row + step, row_count), col) for step in range(1, row_count)]
        + [(row, lax.rem(col + step, col_count)) for step in range(1, col_count)]
    )
    here = pl.ds(pl.multiple_of(place * rows, rows), rows)
    waiting = []

    def launch(*arguments):
        copy = send(*arguments)
        waiting.append(copy)
        return copy

    along_z = {}

    def start_z(node):
        for step in range(1, row_count):
            along_z[node, step] = launch(
                piece.at[node], passed.at[step - 1, node],
                z_send.at[step - 1, node], z_recv.at[step - 1, node],
                lax.rem(row + step, row_count), col,
            )

    delivered = []

    def deliver(step, node):
        source = piece.at[node] if step == 0 else passed.at[step - 1, node]
        target = lax.rem(row - step + row_count, row_count) * groups + group
        remote = pltpu.make_async_remote_copy(
            src_ref=source,
            dst_ref=weights.at[node, here, :],
            send_sem=w_send.at[step, node],
            recv_sem=w_recv.at[place, node],
            device_id=(row, target),
            device_id_type=pl.DeviceIdType.MESH,
        )
        local = pltpu.make_async_copy(source, weights.at[node, here, :], w_send.at[step, node])

        @pl.when(target != col)
        def _():
            remote.start()

        @pl.when(target == col)
        def _():
            local.start()
            local.wait()

        delivered.append((target, remote))

    def arrive(node):
        for slot in range(row_count):
            origin = lax.rem(col, groups) * row_count + slot

            @pl.when(origin != col)
            def _():
                pltpu.make_async_remote_copy(
                    src_ref=piece.at[node],
                    dst_ref=weights.at[node, pl.ds(slot * rows, rows), :],
                    send_sem=w_send.at[0, node],
                    recv_sem=w_recv.at[slot, node],
                    device_id=(row, origin),
                    device_id_type=pl.DeviceIdType.MESH,
                ).wait_recv()

    def padded(node):
        slots = [
            weights[node, pl.ds(member * slot_rows, slot_rows), :].astype(jnp.float32)
            for member in range(CAP)
        ]
        for tile in range(tiles_per_block):
            total = None
            for member in range(CAP):
                line = member * tiles_per_block + tile
                term = slots[member] * chosen[node, pl.ds(line, 1), :]
                total = term if total is None else total + term
            dense[node, pl.ds(tile * slot_rows, slot_rows), :] = total.astype(dense.dtype)

    def product(node, side):
        block = ancestor[:, side, :, :].reshape(mates * panel_rows, ancestor.shape[3])
        total = jnp.dot(block, dense[node], preferred_element_type=jnp.float32)
        return total.reshape(mates, panel_rows, width)

    halves = [pl.ds(0, half_width), pl.ds(half_width, half_width)]

    def view(way, length):
        return (length // 2, 2) if way == 0 else (2, length // 2)

    def at_bit(way, node, value):
        return (node, slice(None), value) if way == 0 else (node, value)

    sums = {}

    def start_sum(node, way, level):
        bit = orders[way][level]
        mine = lax.rem(lax.div(col, bit), 2)
        sums[node, way, level] = launch(
            held[way][level].at[at_bit(way, node, 1 - mine)], came[way][level].at[node],
            rs_send.at[node, way, level], rs_recv.at[node, way, level],
            row, col + (1 - 2 * mine) * bit,
        )

    def end_sum(node, level):
        for way in range(2):
            mine = lax.rem(lax.div(col, orders[way][level]), 2)
            sums[node, way, level].wait_recv()
            value = held[way][level][at_bit(way, node, mine)] + came[way][level][node]
            length = value.shape[0]
            if level + 1 < len(levels):
                held[way][level + 1][node] = value.reshape(view(way, length) + value.shape[1:])
                start_sum(node, way, level + 1)
            else:
                summed[node, :, halves[way]] = value[0]

    own_slots = [0]
    own_steps = bits_of(row_count)[::-1]

    def own_step(number):
        bit = own_steps[number]
        base = len(own_slots) - 1
        copies = []
        for offset, mask in enumerate(own_slots):
            slot = flipped(place, mask, own_steps)
            where = pl.ds(pl.multiple_of(slot * rows, rows), rows)
            target = group * row_count + flipped(place, bit, own_steps)
            copies.append(
                launch(
                    piece if mask == 0 else own.at[:, where, :], own.at[:, where, :],
                    own_send.at[base + offset], own_recv.at[base + offset], row, target,
                )
            )
        own_slots.extend([mask ^ bit for mask in own_slots])
        return copies

    start_z(0)
    deliver(0, 0)
    local = pltpu.make_async_copy(piece, own.at[:, here, :], local_sem)
    local.start()
    own_pending = []
    for node in range(nodes):
        for step in range(1, row_count):
            along_z[node, step].wait_recv()
            deliver(step, node)
            if step == 1 and node + 1 < nodes:
                start_z(node + 1)
                deliver(0, node + 1)
        if node == nodes - 1:
            own_pending = own_step(0)
        arrive(node)
        padded(node)
        given_core[node] = product(node, 1 - core)
        to_core = launch(
            given_core.at[node], core_in.at[node], core_send.at[node], core_recv.at[node],
            row, col + 1 - 2 * core,
        )
        kept = product(node, core)
        for way in range(2):
            part = kept[:, :, way * half_width:(way + 1) * half_width]
            held[way][0][node] = part.reshape(view(way, mates) + part.shape[1:])
        to_core.wait_recv()
        for way in range(2):
            part = core_in[node, :, :, halves[way]]
            held[way][0][node] += part.reshape(view(way, mates) + part.shape[1:])
            start_sum(node, way, 0)
        for earlier in range(node):
            level = node - 1 - earlier
            if level < len(levels):
                end_sum(earlier, level)
    for number in range(1, len(own_steps)):
        for copy in own_pending:
            copy.wait_recv()
        own_pending = own_step(number)
    for turn in range(nodes, nodes + len(levels)):
        for earlier in range(nodes):
            level = turn - 1 - earlier
            if 0 <= level < len(levels):
                end_sum(earlier, level)
    for copy in own_pending:
        copy.wait_recv()
    local.wait()
    for target, remote in delivered:

        @pl.when(target != col)
        def _():
            remote.wait_send()

    for copy in waiting:
        copy.wait_send()


def summed_panels(ancestor, factor_slots, slot_tiles, row_count, col_count):
    nodes, rows, width = factor_slots.shape
    block_rows, block_cols = ancestor.shape
    tiles_per_block = block_cols // TILE
    col = lax.axis_index("col")
    ids = lax.dynamic_slice_in_dim(slot_tiles, col * CAP, CAP, 1) - col * tiles_per_block
    chosen = ids[:, :, None] == jnp.arange(tiles_per_block, dtype=ids.dtype)
    chosen = chosen.reshape(nodes, CAP * tiles_per_block, 1).astype(jnp.float32)
    chosen = jnp.broadcast_to(chosen, (nodes, CAP * tiles_per_block, width))
    mates, panel_rows = col_count // 2, block_rows // col_count
    gathered = (nodes, row_count * rows, width)
    dma = pltpu.SemaphoreType.DMA
    levels = len(bits_of(col_count)) - 1
    vmem, f32, half_width = pltpu.VMEM, jnp.float32, width // 2
    tail = (panel_rows, half_width)
    low = [vmem((nodes, (mates >> j) // 2, 2) + tail, f32) for j in range(levels)]
    high = [vmem((nodes, 2, (mates >> j) // 2) + tail, f32) for j in range(levels)]
    came = [vmem((nodes, (mates >> j) // 2) + tail, f32) for j in range(levels)]
    return pl.pallas_call(
        functools.partial(panels_kernel, row_count, col_count),
        out_shape=(
            jax.ShapeDtypeStruct((nodes, panel_rows, width), f32),
            jax.ShapeDtypeStruct(gathered, factor_slots.dtype),
        ),
        in_specs=[VMEM, VMEM, VMEM],
        out_specs=(VMEM, VMEM),
        scratch_shapes=[
            vmem(gathered, factor_slots.dtype),
            vmem((nodes, block_cols, width), factor_slots.dtype),
            vmem((row_count - 1, nodes, rows, width), factor_slots.dtype),
            vmem((nodes, mates, panel_rows, width), f32),
            vmem((nodes, mates, panel_rows, width), f32),
            dma((row_count - 1, nodes)),
            dma((row_count - 1, nodes)),
            dma((row_count, nodes)),
            dma((row_count, nodes)),
            dma((row_count - 1,)),
            dma((row_count - 1,)),
            dma,
            dma((nodes,)),
            dma((nodes,)),
            dma((nodes, 2, levels)),
            dma((nodes, 2, levels)),
        ] + low + high + came + came,
        compiler_params=pltpu.CompilerParams(
            collective_id=0, has_side_effects=True, vmem_limit_bytes=60 * 2**20
        ),
        name="summed_panels",
    )(chosen, ancestor.reshape(mates, 2, panel_rows, block_cols), factor_slots)


def sum_kernel(orders, bounds, given, out, total, landed, rs_send, rs_recv, ag_send, ag_recv):
    index = {"row": lax.axis_index("row"), "col": lax.axis_index("col")}

    def partner(bit):
        axis, weight = bit
        mine = lax.rem(lax.div(index[axis], weight), 2)
        moved = dict(index)
        moved[axis] = index[axis] + (1 - 2 * mine) * weight
        return mine, moved["row"], moved["col"]

    greet([partner(bit)[1:] for bit in sorted(orders[0])])
    steps = len(orders[0])
    starts = [[base] for base, _ in bounds]
    copies = {}
    landing = [base for base, _ in bounds]

    def rows_at(start, length):
        return pl.ds(pl.multiple_of(start, 8), length)

    def halve(part, step):
        half = bounds[part][1] >> (step + 1)
        mine, row, col = partner(orders[part][step])
        start = starts[part][step]
        source = given if step == 0 else total
        copies[part, step] = send(
            source.at[rows_at(start + (1 - mine) * half, half)],
            landed.at[pl.ds(landing[part], half)],
            rs_send.at[part, step], rs_recv.at[part, step], row, col,
        )
        starts[part].append(start + mine * half)

    def add(part, step):
        half = bounds[part][1] >> (step + 1)
        start = starts[part][step + 1]
        source = given if step == 0 else total
        target = out if step == steps - 1 else total
        chunk = min(half, 32)

        def body(turn, carry):
            rows = rows_at(start + turn * chunk, chunk)
            target[rows, :] = (
                source[rows, :] + landed[rows_at(landing[part] + turn * chunk, chunk), :]
            )
            return carry

        lax.fori_loop(0, half // chunk, body, 0)
        landing[part] += half

    def double(part, step):
        length = bounds[part][1] >> (step + 1)
        _, row, col = partner(orders[part][step])
        where = rows_at(starts[part][step + 1], length)
        copies[part, steps + step] = send(
            out.at[where], out.at[where], ag_send.at[part, step], ag_recv.at[part, step], row, col
        )

    parts = range(len(orders))
    for part in parts:
        halve(part, 0)
    for step in range(steps):
        for part in parts:
            copies[part, step].wait_recv()
            add(part, step)
            if step + 1 < steps:
                halve(part, step + 1)
            else:
                double(part, step)
    for step in range(steps - 1, -1, -1):
        for part in parts:
            half = bounds[part][1] >> (step + 1)
            mine, row, col = partner(orders[part][step])
            pltpu.make_async_remote_copy(
                src_ref=out.at[rows_at(starts[part][step + 1], half)],
                dst_ref=out.at[rows_at(starts[part][step] + (1 - mine) * half, half)],
                send_sem=ag_send.at[part, step],
                recv_sem=ag_recv.at[part, step],
                device_id=(row, col),
                device_id_type=pl.DeviceIdType.MESH,
            ).wait_recv()
            if step > 0:
                double(part, step - 1)
    for copy in copies.values():
        copy.wait_send()


def sum_all(given, row_count, col_count):
    rows, width = given.shape
    col_bits, row_bits = bits_of(col_count), bits_of(row_count)
    half = 1 + (len(col_bits) - 1) // 2
    core = [("col", bit) for bit in col_bits[:1]]
    x = [("col", bit) for bit in col_bits[1:half]]
    y = [("col", bit) for bit in col_bits[half:]]
    z = [("row", bit) for bit in row_bits]
    orders = (core + x + y + z, core + y + x + z, core + z + x + y)
    unit = 8 * row_count * col_count
    units = max(3, -(-rows // unit))
    shares = (-(-units * 2 // 5), -(-units * 2 // 5))
    if units < 5:
        shares = (1, 1)
    shares = shares + (units - sum(shares),)
    bounds, base = [], 0
    for share in shares:
        bounds.append((base, share * unit))
        base += share * unit
    if base > rows:
        given = jnp.concatenate([given, jnp.zeros((base - rows, width), given.dtype)])
    shape = (base, width)
    dma = pltpu.SemaphoreType.DMA((len(orders), len(orders[0])))
    out = pl.pallas_call(
        functools.partial(sum_kernel, orders, bounds),
        out_shape=jax.ShapeDtypeStruct(shape, given.dtype),
        in_specs=[VMEM],
        out_specs=VMEM,
        scratch_shapes=[
            pltpu.VMEM(shape, given.dtype),
            pltpu.VMEM(shape, given.dtype),
            dma, dma, dma, dma,
        ],
        compiler_params=pltpu.CompilerParams(
            collective_id=1, has_side_effects=True, vmem_limit_bytes=56 * 2**20
        ),
        name="sum_all",
    )(given)
    return out[:rows]


def padded_block(slot_data, slot_ids, block_index, tiles_per_block, tile_rows):
    local_tile = slot_ids - block_index * tiles_per_block
    pieces = []
    for tile_index in range(tiles_per_block):
        chosen = jnp.zeros((tile_rows, slot_data.shape[1]), slot_data.dtype)
        for member in range(slot_ids.shape[0]):
            chosen = jnp.where(
                local_tile[member] == tile_index,
                slot_data[member * tile_rows : (member + 1) * tile_rows],
                chosen,
            )
        pieces.append(chosen)
    return jnp.concatenate(pieces, axis=0)


def on_device(ancestor_inverse, factor_slots, slot_tiles, parent_factor, diag_inverse):
    row_count = lax.axis_size("row")
    col_count = lax.axis_size("col")
    row_index = lax.axis_index("row")
    col_index = lax.axis_index("col")
    block_rows, block_cols = ancestor_inverse.shape
    tile_rows = TILE
    tiles_per_block = block_cols // tile_rows
    node_count = factor_slots.shape[0]
    panel_width = factor_slots.shape[2]
    slot_count = CAP
    groups_per_row = col_count // row_count
    panel_rows = block_rows // col_count
    own_block = row_index * groups_per_row + col_index // row_count
    own_offset = col_index % row_count * panel_rows

    def own_part(node, own_slots):
        own_ids = lax.dynamic_slice_in_dim(
            slot_tiles[node], own_block * slot_count, slot_count
        )
        own_padded = padded_block(own_slots, own_ids, own_block, tiles_per_block, tile_rows)
        own_rows = lax.dynamic_slice_in_dim(own_padded, own_offset, panel_rows, 0)
        return own_rows.astype(jnp.float32)

    def finish(node, first_total, second_total, prev_diag):
        if node == 0:
            return (diag_inverse[0] - first_total, None)
        parent_link = parent_factor[node - 1].astype(jnp.float32)
        upper = -(second_total + jnp.dot(prev_diag, parent_link, precision=exact_mode))
        diagonal = (
            diag_inverse[node] - first_total - jnp.dot(parent_link.T, upper, precision=exact_mode)
        )
        return (diagonal, upper)

    panels = []
    diagonals = []
    parents = []
    summed_all, own_all = summed_panels(
        ancestor_inverse, factor_slots, slot_tiles, row_count, col_count
    )
    firsts = []
    previous = None
    seconds = []
    for node in range(node_count):
        own_rows = own_part(node, own_all[node])
        column = -summed_all[node]
        if node > 0:
            advance_parent_link = parent_factor[node - 1].astype(jnp.float32)
            column = column - jnp.dot(previous, advance_parent_link, precision=exact_mode)
        if node > 0:
            seconds.append(jnp.dot(previous.T, own_rows, precision=exact_mode))
        firsts.append(jnp.dot(own_rows.T, column, precision=exact_mode))
        panels.append(column.astype(jnp.bfloat16))
        previous = column
    totals = sum_all(jnp.concatenate(firsts + seconds, axis=0), row_count, col_count)
    totals = totals.reshape(-1, panel_width, panel_width)
    first_totals, second_totals = totals[:node_count], totals[node_count:]
    prev_diag = None
    for node in range(node_count):
        second_total = second_totals[node - 1] if node > 0 else None
        diagonal, upper = finish(node, first_totals[node], second_total, prev_diag)
        diagonals.append(diagonal)
        if node > 0:
            parents.append(upper)
        prev_diag = diagonal
    return (jnp.stack(panels), jnp.stack(diagonals), jnp.stack(parents))


def solution(mesh):
    placed = (P("row", "col"), P(None, ("row", "col"), None), P(), P(), P())
    return jax.shard_map(
        on_device,
        mesh=mesh,
        in_specs=placed,
        out_specs=(P(None, ("row", "col"), None), P(), P()),
        check_vma=False,
    )
```

```python
import functools

import jax
import jax.numpy as jnp
from jax import lax
from jax.experimental import pallas as pl
from jax.experimental.pallas import tpu as pltpu
from jax.sharding import PartitionSpec as P

TILE = 256
CAP = 2
MERGED_SIZE = 1536 * 512


exact_mode = lax.Precision.HIGHEST


VMEM = pl.BlockSpec(memory_space=pltpu.VMEM)


def send(src, dst, send_sem, recv_sem, row, col):
    copy = pltpu.make_async_remote_copy(
        src_ref=src,
        dst_ref=dst,
        send_sem=send_sem,
        recv_sem=recv_sem,
        device_id=(row, col),
        device_id_type=pl.DeviceIdType.MESH,
    )
    copy.start()
    return copy


def greet(peers):
    barrier = pltpu.get_barrier_semaphore()
    for row, col in peers:
        pl.semaphore_signal(
            barrier, inc=1, device_id=(row, col), device_id_type=pl.DeviceIdType.MESH
        )
    pl.semaphore_wait(barrier, len(peers))


def bits_of(count):
    return [1 << place for place in range(count.bit_length() - 1)]


def flipped(place, mask, bits):
    for bit in bits:
        if mask & bit:
            place = place + (1 - 2 * lax.rem(lax.div(place, bit), 2)) * bit
    return place


def split(value):
    parts = []
    for _ in range(3):
        part = value.astype(jnp.bfloat16)
        parts.append(part)
        value = value - part.astype(jnp.float32)
    return parts


def times(left, right, left_dim, right_dim):
    total = None
    lefts = split(left) if left.dtype == jnp.float32 else [left]
    rights = split(right) if right.dtype == jnp.float32 else [right]
    for one in lefts:
        for other in rights:
            term = lax.dot_general(
                one, other, (((left_dim,), (right_dim,)), ((), ())),
                preferred_element_type=jnp.float32,
            )
            total = term if total is None else total + term
    return total


LANES = 128


def put(ref, part, value):
    rows, width = value.shape
    for turn in range(width // LANES):
        ref[part, pl.ds(turn * rows, rows), :] = value[:, turn * LANES:(turn + 1) * LANES]


def get(ref, part, width):
    rows = ref.shape[1] * LANES // width
    return jnp.concatenate(
        [ref[part, pl.ds(turn * rows, rows), :] for turn in range(width // LANES)], axis=1
    )


def whole_kernel(row_count, col_count, merged, *refs):
    chosen, chosen_own, ancestor, piece, links, diag_inverse, panels = refs[:7]
    if merged:
        diags, parents, acc, landed, gathered, s_send, s_recv, g_send, g_recv = refs[7:16]
        own, summed, *scratch = refs[16:]
    else:
        acc = refs[7]
        own, summed, *scratch = refs[8:]
    (weights, dense, passed, given_core, core_in, z_send, z_recv, w_send, w_recv, own_send, own_recv,
     local_sem, core_send, core_recv, rs_send, rs_recv) = scratch[:16]
    levels = bits_of(col_count)[1:]
    held = [scratch[16:16 + len(levels)], scratch[16 + len(levels):16 + 2 * len(levels)]]
    rest = scratch[16 + 2 * len(levels):]
    came = [rest[:len(levels)], rest[len(levels):]]
    orders = [levels, levels[::-1]]
    row, col = lax.axis_index("row"), lax.axis_index("col")
    groups = col_count // row_count
    nodes, rows, width = piece.shape
    half_width = width // 2
    place, group = lax.rem(col, row_count), lax.div(col, row_count)
    core = lax.rem(col, 2)
    mates, panel_rows = ancestor.shape[0], ancestor.shape[2]
    slot_rows = TILE
    tiles_per_block = ancestor.shape[3] // slot_rows
    greet(
        [(lax.rem(row + step, row_count), col) for step in range(1, row_count)]
        + [(row, lax.rem(col + step, col_count)) for step in range(1, col_count)]
    )
    here = pl.ds(pl.multiple_of(place * rows, rows), rows)
    waiting = []

    def launch(*arguments):
        copy = send(*arguments)
        waiting.append(copy)
        return copy

    along_z = {}

    def start_z(node):
        for step in range(1, row_count):
            along_z[node, step] = launch(
                piece.at[node], passed.at[step - 1, node],
                z_send.at[step - 1, node], z_recv.at[step - 1, node],
                lax.rem(row + step, row_count), col,
            )

    delivered = []

    def deliver(step, node):
        source = piece.at[node] if step == 0 else passed.at[step - 1, node]
        target = lax.rem(row - step + row_count, row_count) * groups + group
        remote = pltpu.make_async_remote_copy(
            src_ref=source,
            dst_ref=weights.at[node, here, :],
            send_sem=w_send.at[step, node],
            recv_sem=w_recv.at[place, node],
            device_id=(row, target),
            device_id_type=pl.DeviceIdType.MESH,
        )
        local = pltpu.make_async_copy(source, weights.at[node, here, :], w_send.at[step, node])

        @pl.when(target != col)
        def _():
            remote.start()

        @pl.when(target == col)
        def _():
            local.start()
            local.wait()

        delivered.append((target, remote))

    def arrive(node):
        for slot in range(row_count):
            origin = lax.rem(col, groups) * row_count + slot

            @pl.when(origin != col)
            def _():
                pltpu.make_async_remote_copy(
                    src_ref=piece.at[node],
                    dst_ref=weights.at[node, pl.ds(slot * rows, rows), :],
                    send_sem=w_send.at[0, node],
                    recv_sem=w_recv.at[slot, node],
                    device_id=(row, origin),
                    device_id_type=pl.DeviceIdType.MESH,
                ).wait_recv()

    def padded(node, slots_ref, marks):
        slots = [
            slots_ref[node, pl.ds(member * slot_rows, slot_rows), :].astype(jnp.float32)
            for member in range(CAP)
        ]
        for tile in range(tiles_per_block):
            total = None
            for member in range(CAP):
                line = member * tiles_per_block + tile
                term = slots[member] * marks[node, pl.ds(line, 1), :]
                total = term if total is None else total + term
            dense[node, pl.ds(tile * slot_rows, slot_rows), :] = total.astype(dense.dtype)

    def product(node, side):
        block = ancestor[:, side, :, :].reshape(mates * panel_rows, ancestor.shape[3])
        total = jnp.dot(block, dense[node], preferred_element_type=jnp.float32)
        return total.reshape(mates, panel_rows, width)

    halves = [pl.ds(0, half_width), pl.ds(half_width, half_width)]

    def view(way, length):
        return (length // 2, 2) if way == 0 else (2, length // 2)

    def at_bit(way, node, value):
        return (node, slice(None), value) if way == 0 else (node, value)

    sums = {}

    def start_sum(node, way, level):
        bit = orders[way][level]
        mine = lax.rem(lax.div(col, bit), 2)
        sums[node, way, level] = launch(
            held[way][level].at[at_bit(way, node, 1 - mine)], came[way][level].at[node],
            rs_send.at[node, way, level], rs_recv.at[node, way, level],
            row, col + (1 - 2 * mine) * bit,
        )

    def end_sum(node, level):
        for way in range(2):
            mine = lax.rem(lax.div(col, orders[way][level]), 2)
            sums[node, way, level].wait_recv()
            value = held[way][level][at_bit(way, node, mine)] + came[way][level][node]
            length = value.shape[0]
            if level + 1 < len(levels):
                held[way][level + 1][node] = value.reshape(view(way, length) + value.shape[1:])
                start_sum(node, way, level + 1)
            else:
                summed[node, :, halves[way]] = value[0]

    own_slots = [0]
    own_steps = bits_of(row_count)[::-1]

    def own_step(number):
        bit = own_steps[number]
        base = len(own_slots) - 1
        copies = []
        for offset, mask in enumerate(own_slots):
            slot = flipped(place, mask, own_steps)
            where = pl.ds(pl.multiple_of(slot * rows, rows), rows)
            target = group * row_count + flipped(place, bit, own_steps)
            copies.append(
                launch(
                    piece if mask == 0 else own.at[:, where, :], own.at[:, where, :],
                    own_send.at[base + offset], own_recv.at[base + offset], row, target,
                )
            )
        own_slots.extend([mask ^ bit for mask in own_slots])
        return copies

    parts = 2 * nodes - 1
    first_of = [0] + [2 * node - 1 for node in range(1, nodes)]
    index = {"row": row, "col": col}
    col_bits, row_bits = bits_of(col_count), bits_of(row_count)
    middle = 1 + (len(col_bits) - 1) // 2
    c_bits = [("col", bit) for bit in col_bits[:1]]
    x_bits = [("col", bit) for bit in col_bits[1:middle]]
    y_bits = [("col", bit) for bit in col_bits[middle:]]
    z_bits = [("row", bit) for bit in row_bits]
    ways = [c_bits + z_bits + x_bits + y_bits]
    for part in range(1, parts):
        ways.append(c_bits + (x_bits + y_bits if part % 2 else y_bits + x_bits) + z_bits)
    steps = len(ways[0])
    size = acc.shape[1]
    starts = [[0] for _ in range(parts)]
    at_step = [None] * parts
    flying = {}

    def partner(bit):
        axis, weight = bit
        mine = lax.rem(lax.div(index[axis], weight), 2)
        moved = dict(index)
        moved[axis] = index[axis] + (1 - 2 * mine) * weight
        return mine, moved["row"], moved["col"]

    def rows_at(start, length):
        return pl.ds(pl.multiple_of(start, 8), length)

    def landing(step):
        return size - (size >> step)

    def halve(part, step):
        half = size >> (step + 1)
        mine, to_row, to_col = partner(ways[part][step])
        start = starts[part][step]
        flying[part, step] = launch(
            acc.at[part, rows_at(start + (1 - mine) * half, half)],
            landed.at[part, pl.ds(landing(step), half)],
            s_send.at[part, step], s_recv.at[part, step], to_row, to_col,
        )
        starts[part].append(start + mine * half)

    def add(part, step):
        half = size >> (step + 1)
        start = starts[part][step + 1]
        target = gathered if step == steps - 1 else acc
        chunk = min(half, 256)

        def body(turn, carry):
            where = rows_at(start + turn * chunk, chunk)
            target[part, where, :] = (
                acc[part, where, :]
                + landed[part, rows_at(landing(step) + turn * chunk, chunk), :]
            )
            return carry

        lax.fori_loop(0, half // chunk, body, 0)

    def double(part, step):
        length = size >> (step + 1)
        _, to_row, to_col = partner(ways[part][step])
        where = rows_at(starts[part][step + 1], length)
        launch(
            gathered.at[part, where], gathered.at[part, where],
            g_send.at[part, step], g_recv.at[part, step], to_row, to_col,
        )

    def begin(part):
        if merged:
            at_step[part] = 0
            halve(part, 0)

    def advance(part):
        now = at_step[part]
        if now is None or now == 2 * steps:
            return
        at_step[part] = now + 1
        if now < steps:
            flying[part, now].wait_recv()
            add(part, now)
            if now + 1 < steps:
                halve(part, now + 1)
            else:
                double(part, now)
            return
        step = 2 * steps - 1 - now
        half = size >> (step + 1)
        mine, to_row, to_col = partner(ways[part][step])
        pltpu.make_async_remote_copy(
            src_ref=gathered.at[part, rows_at(starts[part][step + 1], half)],
            dst_ref=gathered.at[part, rows_at(starts[part][step] + (1 - mine) * half, half)],
            send_sem=g_send.at[part, step],
            recv_sem=g_recv.at[part, step],
            device_id=(to_row, to_col),
            device_id_type=pl.DeviceIdType.MESH,
        ).wait_recv()
        if step > 0:
            double(part, step - 1)

    def finish_node(node):
        column = -summed[node]
        if node > 0:
            column = column - times(summed[node - 1], links[node - 1], 1, 0)
        panels[node] = column.astype(panels.dtype)
        padded(node, own, chosen_own)
        own_rows = dense[
            node, pl.ds(pl.multiple_of(place * panel_rows, 16), panel_rows), :
        ]
        put(acc, first_of[node], times(own_rows, column, 0, 0))
        begin(first_of[node])
        if node > 0:
            put(acc, first_of[node] + 1, times(summed[node - 1], own_rows, 0, 0))
            begin(first_of[node] + 1)
        summed[node] = column

    def last_steps(node):
        first = get(gathered, first_of[node], width)
        if node == 0:
            diags[0] = diag_inverse[0] - first
            return
        second = get(gathered, first_of[node] + 1, width)
        parents[node - 1] = -(second + times(diags[node - 1], links[node - 1], 1, 0))
        diags[node] = diag_inverse[node] - first - times(links[node - 1], parents[node - 1], 0, 0)

    start_z(0)
    deliver(0, 0)
    local = pltpu.make_async_copy(piece, own.at[:, here, :], local_sem)
    local.start()
    own_pending = []
    to_core = None
    finished = []

    def next_own():
        for copy in own_pending:
            copy.wait_recv()
        own_pending.clear()
        if len(own_slots) < row_count:
            own_pending.extend(own_step(bits_of(row_count).index(len(own_slots))))

    def turn_sums(turn):
        for earlier in range(min(turn, nodes)):
            level = turn - 1 - earlier
            if level < len(levels):
                end_sum(earlier, level)
                if level == len(levels) - 1:
                    while own_pending or len(own_slots) < row_count:
                        next_own()
                    if not finished:
                        local.wait()
                    finish_node(earlier)
                    finished.append(earlier)

    for node in range(nodes):
        for step in range(1, row_count):
            along_z[node, step].wait_recv()
            deliver(step, node)
            if step == 1 and node + 1 < nodes:
                start_z(node + 1)
                deliver(0, node + 1)
        next_own()
        arrive(node)
        padded(node, weights, chosen)
        if to_core is not None:
            to_core.wait_send()
        given_core[...] = product(node, 1 - core)
        to_core = send(
            given_core, core_in.at[node], core_send.at[node], core_recv.at[node],
            row, col + 1 - 2 * core,
        )
        kept = product(node, core)
        for way in range(2):
            part = kept[:, :, way * half_width:(way + 1) * half_width]
            held[way][0][node] = part.reshape(view(way, mates) + part.shape[1:])
        to_core.wait_recv()
        for way in range(2):
            part = core_in[node, :, :, halves[way]]
            held[way][0][node] += part.reshape(view(way, mates) + part.shape[1:])
            start_sum(node, way, 0)
        turn_sums(node)
    for turn in range(nodes, nodes + len(levels)):
        for part in range(parts):
            advance(part)
        turn_sums(turn)
    to_core.wait_send()
    if merged:
        ended = 0
        while ended < nodes:
            for part in range(parts):
                advance(part)
            while ended < nodes and all(
                at_step[part] == 2 * steps for part in range(first_of[ended] + (2 if ended else 1))
            ):
                last_steps(ended)
                ended += 1
    for target, remote in delivered:

        @pl.when(target != col)
        def _():
            remote.wait_send()

    for copy in waiting:
        copy.wait_send()


def marks(slot_tiles, block, tiles_per_block, width):
    ids = lax.dynamic_slice_in_dim(slot_tiles, block * CAP, CAP, 1) - block * tiles_per_block
    chosen = ids[:, :, None] == jnp.arange(tiles_per_block, dtype=ids.dtype)
    chosen = chosen.reshape(-1, CAP * tiles_per_block, 1).astype(jnp.float32)
    return jnp.broadcast_to(chosen, chosen.shape[:2] + (width,))


def run_kernel(
    merged, ancestor, factor_slots, slot_tiles, parent_factor, diag_inverse, row_count, col_count
):
    nodes, rows, width = factor_slots.shape
    block_rows, block_cols = ancestor.shape
    tiles_per_block = block_cols // TILE
    row, col = lax.axis_index("row"), lax.axis_index("col")
    own_block = row * (col_count // row_count) + col // row_count
    mates, panel_rows = col_count // 2, block_rows // col_count
    gathered = (nodes, row_count * rows, width)
    dma = pltpu.SemaphoreType.DMA
    levels = len(bits_of(col_count)) - 1
    vmem, f32, half_width = pltpu.VMEM, jnp.float32, width // 2
    tail = (panel_rows, half_width)
    low = [vmem((nodes, (mates >> j) // 2, 2) + tail, f32) for j in range(levels)]
    high = [vmem((nodes, 2, (mates >> j) // 2) + tail, f32) for j in range(levels)]
    came = [vmem((nodes, (mates >> j) // 2) + tail, f32) for j in range(levels)]
    parts, steps = 2 * nodes - 1, len(bits_of(row_count)) + len(bits_of(col_count))
    sums = (parts, width * width // LANES, LANES)
    out_shape = [jax.ShapeDtypeStruct((nodes, panel_rows, width), factor_slots.dtype)]
    extra = []
    if merged:
        out_shape += [
            jax.ShapeDtypeStruct((nodes, width, width), f32),
            jax.ShapeDtypeStruct((nodes - 1, width, width), f32),
        ]
        extra = [vmem(sums, f32)] * 3 + [dma((parts, steps))] * 4
    else:
        out_shape += [jax.ShapeDtypeStruct(sums, f32)]
    return pl.pallas_call(
        functools.partial(whole_kernel, row_count, col_count, merged),
        out_shape=out_shape,
        in_specs=[VMEM] * 5 + [VMEM if merged else pl.BlockSpec(memory_space=pl.ANY)],
        out_specs=[VMEM] * len(out_shape),
        scratch_shapes=extra + [
            vmem(gathered, factor_slots.dtype),
            vmem((nodes, panel_rows, width), f32),
            vmem(gathered, factor_slots.dtype),
            vmem((nodes, block_cols, width), factor_slots.dtype),
            vmem((row_count - 1, nodes, rows, width), factor_slots.dtype),
            vmem((mates, panel_rows, width), f32),
            vmem((nodes, mates, panel_rows, width), f32),
            dma((row_count - 1, nodes)),
            dma((row_count - 1, nodes)),
            dma((row_count, nodes)),
            dma((row_count, nodes)),
            dma((row_count - 1,)),
            dma((row_count - 1,)),
            dma,
            dma((nodes,)),
            dma((nodes,)),
            dma((nodes, 2, levels)),
            dma((nodes, 2, levels)),
        ] + low + high + came + came,
        compiler_params=pltpu.CompilerParams(
            collective_id=0, has_side_effects=True, vmem_limit_bytes=61 * 2**20
        ),
        name="selected_inverse",
    )(
        marks(slot_tiles, col, tiles_per_block, width),
        marks(slot_tiles, own_block, tiles_per_block, width),
        ancestor.reshape(mates, 2, panel_rows, block_cols),
        factor_slots, parent_factor, diag_inverse,
    )


def sum_kernel(orders, bounds, given, out, total, landed, rs_send, rs_recv, ag_send, ag_recv):
    index = {"row": lax.axis_index("row"), "col": lax.axis_index("col")}

    def partner(bit):
        axis, weight = bit
        mine = lax.rem(lax.div(index[axis], weight), 2)
        moved = dict(index)
        moved[axis] = index[axis] + (1 - 2 * mine) * weight
        return mine, moved["row"], moved["col"]

    greet([partner(bit)[1:] for bit in sorted(orders[0])])
    steps = len(orders[0])
    starts = [[base] for base, _ in bounds]
    copies = {}
    landing = [base for base, _ in bounds]

    def rows_at(start, length):
        return pl.ds(pl.multiple_of(start, 8), length)

    def halve(part, step):
        half = bounds[part][1] >> (step + 1)
        mine, row, col = partner(orders[part][step])
        start = starts[part][step]
        source = given if step == 0 else total
        copies[part, step] = send(
            source.at[rows_at(start + (1 - mine) * half, half)],
            landed.at[pl.ds(landing[part], half)],
            rs_send.at[part, step], rs_recv.at[part, step], row, col,
        )
        starts[part].append(start + mine * half)

    def add(part, step):
        half = bounds[part][1] >> (step + 1)
        start = starts[part][step + 1]
        source = given if step == 0 else total
        target = out if step == steps - 1 else total
        chunk = min(half, 32)

        def body(turn, carry):
            rows = rows_at(start + turn * chunk, chunk)
            target[rows, :] = (
                source[rows, :] + landed[rows_at(landing[part] + turn * chunk, chunk), :]
            )
            return carry

        lax.fori_loop(0, half // chunk, body, 0)
        landing[part] += half

    def double(part, step):
        length = bounds[part][1] >> (step + 1)
        _, row, col = partner(orders[part][step])
        where = rows_at(starts[part][step + 1], length)
        copies[part, steps + step] = send(
            out.at[where], out.at[where], ag_send.at[part, step], ag_recv.at[part, step], row, col
        )

    parts = range(len(orders))
    for part in parts:
        halve(part, 0)
    for step in range(steps):
        for part in parts:
            copies[part, step].wait_recv()
            add(part, step)
            if step + 1 < steps:
                halve(part, step + 1)
            else:
                double(part, step)
    for step in range(steps - 1, -1, -1):
        for part in parts:
            half = bounds[part][1] >> (step + 1)
            mine, row, col = partner(orders[part][step])
            pltpu.make_async_remote_copy(
                src_ref=out.at[rows_at(starts[part][step + 1], half)],
                dst_ref=out.at[rows_at(starts[part][step] + (1 - mine) * half, half)],
                send_sem=ag_send.at[part, step],
                recv_sem=ag_recv.at[part, step],
                device_id=(row, col),
                device_id_type=pl.DeviceIdType.MESH,
            ).wait_recv()
            if step > 0:
                double(part, step - 1)
    for copy in copies.values():
        copy.wait_send()


def sum_all(given, row_count, col_count):
    rows, width = given.shape
    col_bits, row_bits = bits_of(col_count), bits_of(row_count)
    half = 1 + (len(col_bits) - 1) // 2
    core = [("col", bit) for bit in col_bits[:1]]
    x = [("col", bit) for bit in col_bits[1:half]]
    y = [("col", bit) for bit in col_bits[half:]]
    z = [("row", bit) for bit in row_bits]
    orders = (core + x + y + z, core + y + x + z, core + z + x + y)
    unit = 8 * row_count * col_count
    units = max(3, -(-rows // unit))
    shares = (-(-units * 2 // 5), -(-units * 2 // 5))
    if units < 5:
        shares = (1, 1)
    shares = shares + (units - sum(shares),)
    bounds, base = [], 0
    for share in shares:
        bounds.append((base, share * unit))
        base += share * unit
    if base > rows:
        given = jnp.concatenate([given, jnp.zeros((base - rows, width), given.dtype)])
    shape = (base, width)
    dma = pltpu.SemaphoreType.DMA((len(orders), len(orders[0])))
    out = pl.pallas_call(
        functools.partial(sum_kernel, orders, bounds),
        out_shape=jax.ShapeDtypeStruct(shape, given.dtype),
        in_specs=[VMEM],
        out_specs=VMEM,
        scratch_shapes=[
            pltpu.VMEM(shape, given.dtype),
            pltpu.VMEM(shape, given.dtype),
            dma, dma, dma, dma,
        ],
        compiler_params=pltpu.CompilerParams(
            collective_id=1, has_side_effects=True, vmem_limit_bytes=56 * 2**20
        ),
        name="sum_all",
    )(given)
    return out[:rows]


def on_device(ancestor_inverse, factor_slots, slot_tiles, parent_factor, diag_inverse):
    row_count = lax.axis_size("row")
    col_count = lax.axis_size("col")
    nodes, _, width = factor_slots.shape
    merged = ancestor_inverse.shape[0] * width <= MERGED_SIZE
    results = run_kernel(
        merged, ancestor_inverse, factor_slots, slot_tiles, parent_factor, diag_inverse,
        row_count, col_count,
    )
    if merged:
        return tuple(results)
    panels, sums = results
    sums = sums.reshape(2 * nodes - 1, -1, width, LANES).transpose(0, 2, 1, 3)
    totals = sum_all(sums.reshape(-1, width), row_count, col_count)
    totals = totals.reshape(-1, width, width)
    diagonals = [diag_inverse[0] - totals[0]]
    parents = []
    for node in range(1, nodes):
        link = parent_factor[node - 1].astype(jnp.float32)
        upper = -(
            totals[2 * node] + jnp.dot(diagonals[-1], link, precision=exact_mode)
        )
        parents.append(upper)
        diagonals.append(
            diag_inverse[node] - totals[2 * node - 1]
            - jnp.dot(link.T, upper, precision=exact_mode)
        )
    return panels, jnp.stack(diagonals), jnp.stack(parents)


def solution(mesh):
    placed = (P("row", "col"), P(None, ("row", "col"), None), P(), P(), P())
    return jax.shard_map(
        on_device,
        mesh=mesh,
        in_specs=placed,
        out_specs=(P(None, ("row", "col"), None), P(), P()),
        check_vma=False,
    )
```

```python
import functools

import jax
import jax.numpy as jnp
from jax import lax
from jax.experimental import pallas as pl
from jax.experimental.pallas import tpu as pltpu
from jax.sharding import PartitionSpec as P

TILE = 256
CAP = 2
MERGED_SIZE = 1536 * 512


exact_mode = lax.Precision.HIGHEST


VMEM = pl.BlockSpec(memory_space=pltpu.VMEM)
ANY = pl.BlockSpec(memory_space=pl.ANY)


def send(src, dst, send_sem, recv_sem, row, col):
    copy = pltpu.make_async_remote_copy(
        src_ref=src,
        dst_ref=dst,
        send_sem=send_sem,
        recv_sem=recv_sem,
        device_id=(row, col),
        device_id_type=pl.DeviceIdType.MESH,
    )
    copy.start()
    return copy


def greet(peers):
    barrier = pltpu.get_barrier_semaphore()
    for row, col in peers:
        pl.semaphore_signal(
            barrier, inc=1, device_id=(row, col), device_id_type=pl.DeviceIdType.MESH
        )
    pl.semaphore_wait(barrier, len(peers))


def bits_of(count):
    return [1 << place for place in range(count.bit_length() - 1)]


def flipped(place, mask, bits):
    for bit in bits:
        if mask & bit:
            place = place + (1 - 2 * lax.rem(lax.div(place, bit), 2)) * bit
    return place


def split(value):
    parts = []
    for _ in range(3):
        part = value.astype(jnp.bfloat16)
        parts.append(part)
        value = value - part.astype(jnp.float32)
    return parts


def times(left, right, left_dim, right_dim):
    total = None
    lefts = split(left) if left.dtype == jnp.float32 else [left]
    rights = split(right) if right.dtype == jnp.float32 else [right]
    for one in lefts:
        for other in rights:
            term = lax.dot_general(
                one, other, (((left_dim,), (right_dim,)), ((), ())),
                preferred_element_type=jnp.float32,
            )
            total = term if total is None else total + term
    return total


LANES = 128


def put(ref, part, value):
    rows, width = value.shape
    for turn in range(width // LANES):
        ref[part, pl.ds(turn * rows, rows), :] = value[:, turn * LANES:(turn + 1) * LANES]


def get(ref, part, width):
    rows = ref.shape[1] * LANES // width
    return jnp.concatenate(
        [ref[part, pl.ds(turn * rows, rows), :] for turn in range(width // LANES)], axis=1
    )


def whole_kernel(row_count, col_count, merged, *refs):
    chosen, chosen_own, ancestor_given, piece, links, diag_inverse, panels = refs[:7]
    if merged:
        diags, parents, acc, landed, gathered, s_send, s_recv, g_send, g_recv = refs[7:16]
        ancestor, ancestor_sem, diag_sem, own, summed, *scratch = refs[16:]
    else:
        acc = refs[7]
        ancestor, ancestor_sem, diag_sem, own, summed, *scratch = refs[8:]
    (weights, dense, passed, given_core, core_in, z_send, z_recv, w_send, w_recv, own_send, own_recv,
     local_sem, core_send, core_recv, rs_send, rs_recv) = scratch[:16]
    levels = bits_of(col_count)[1:]
    held = [scratch[16:16 + len(levels)], scratch[16 + len(levels):16 + 2 * len(levels)]]
    rest = scratch[16 + 2 * len(levels):]
    came = [rest[:len(levels)], rest[len(levels):]]
    orders = [levels, levels[::-1]]
    row, col = lax.axis_index("row"), lax.axis_index("col")
    groups = col_count // row_count
    nodes, rows, width = piece.shape
    half_width = width // 2
    place, group = lax.rem(col, row_count), lax.div(col, row_count)
    core = lax.rem(col, 2)
    mates, panel_rows = ancestor.shape[0], ancestor.shape[2]
    slot_rows = TILE
    tiles_per_block = ancestor.shape[3] // slot_rows
    greet(
        [(lax.rem(row + step, row_count), col) for step in range(1, row_count)]
        + [(row, lax.rem(col + step, col_count)) for step in range(1, col_count)]
    )
    here = pl.ds(pl.multiple_of(place * rows, rows), rows)
    waiting = []

    def launch(*arguments):
        copy = send(*arguments)
        waiting.append(copy)
        return copy

    along_z = {}

    def start_z(node):
        for step in range(1, row_count):
            along_z[node, step] = launch(
                piece.at[node], passed.at[step - 1, node],
                z_send.at[step - 1, node], z_recv.at[step - 1, node],
                lax.rem(row + step, row_count), col,
            )

    delivered = []

    def deliver(step, node):
        source = piece.at[node] if step == 0 else passed.at[step - 1, node]
        target = lax.rem(row - step + row_count, row_count) * groups + group
        remote = pltpu.make_async_remote_copy(
            src_ref=source,
            dst_ref=weights.at[node, here, :],
            send_sem=w_send.at[step, node],
            recv_sem=w_recv.at[place, node],
            device_id=(row, target),
            device_id_type=pl.DeviceIdType.MESH,
        )
        local = pltpu.make_async_copy(source, weights.at[node, here, :], w_send.at[step, node])

        @pl.when(target != col)
        def _():
            remote.start()

        @pl.when(target == col)
        def _():
            local.start()
            local.wait()

        delivered.append((target, remote))

    def arrive(node):
        for slot in range(row_count):
            origin = lax.rem(col, groups) * row_count + slot

            @pl.when(origin != col)
            def _():
                pltpu.make_async_remote_copy(
                    src_ref=piece.at[node],
                    dst_ref=weights.at[node, pl.ds(slot * rows, rows), :],
                    send_sem=w_send.at[0, node],
                    recv_sem=w_recv.at[slot, node],
                    device_id=(row, origin),
                    device_id_type=pl.DeviceIdType.MESH,
                ).wait_recv()

    def padded(node, slots_ref, marks):
        slots = [
            slots_ref[node, pl.ds(member * slot_rows, slot_rows), :].astype(jnp.float32)
            for member in range(CAP)
        ]
        lines = [
            jnp.concatenate([marks[node, pl.ds(line, 1), :]] * (width // LANES), axis=1)
            for line in range(CAP * tiles_per_block)
        ]
        for tile in range(tiles_per_block):
            total = None
            for member in range(CAP):
                line = member * tiles_per_block + tile
                term = slots[member] * lines[line]
                total = term if total is None else total + term
            dense[node, pl.ds(tile * slot_rows, slot_rows), :] = total.astype(dense.dtype)

    def product(node, side):
        block = ancestor[:, side, :, :].reshape(mates * panel_rows, ancestor.shape[3])
        total = jnp.dot(block, dense[node], preferred_element_type=jnp.float32)
        return total.reshape(mates, panel_rows, width)

    halves = [pl.ds(0, half_width), pl.ds(half_width, half_width)]

    def view(way, length):
        return (length // 2, 2) if way == 0 else (2, length // 2)

    def at_bit(way, node, value):
        return (node, slice(None), value) if way == 0 else (node, value)

    sums = {}

    def start_sum(node, way, level):
        bit = orders[way][level]
        mine = lax.rem(lax.div(col, bit), 2)
        sums[node, way, level] = launch(
            held[way][level].at[at_bit(way, node, 1 - mine)], came[way][level].at[node],
            rs_send.at[node, way, level], rs_recv.at[node, way, level],
            row, col + (1 - 2 * mine) * bit,
        )

    def end_sum(node, level):
        for way in range(2):
            mine = lax.rem(lax.div(col, orders[way][level]), 2)
            sums[node, way, level].wait_recv()
            value = held[way][level][at_bit(way, node, mine)] + came[way][level][node]
            length = value.shape[0]
            if level + 1 < len(levels):
                held[way][level + 1][node] = value.reshape(view(way, length) + value.shape[1:])
                start_sum(node, way, level + 1)
            else:
                summed[node, :, halves[way]] = value[0]

    own_slots = [0]
    own_steps = bits_of(row_count)[::-1]

    def own_step(number):
        bit = own_steps[number]
        base = len(own_slots) - 1
        copies = []
        for offset, mask in enumerate(own_slots):
            slot = flipped(place, mask, own_steps)
            where = pl.ds(pl.multiple_of(slot * rows, rows), rows)
            target = group * row_count + flipped(place, bit, own_steps)
            copies.append(
                launch(
                    piece if mask == 0 else own.at[:, where, :], own.at[:, where, :],
                    own_send.at[base + offset], own_recv.at[base + offset], row, target,
                )
            )
        own_slots.extend([mask ^ bit for mask in own_slots])
        return copies

    parts = 2 * nodes - 1
    first_of = [0] + [2 * node - 1 for node in range(1, nodes)]
    index = {"row": row, "col": col}
    col_bits, row_bits = bits_of(col_count), bits_of(row_count)
    middle = 1 + (len(col_bits) - 1) // 2
    c_bits = [("col", bit) for bit in col_bits[:1]]
    x_bits = [("col", bit) for bit in col_bits[1:middle]]
    y_bits = [("col", bit) for bit in col_bits[middle:]]
    z_bits = [("row", bit) for bit in row_bits]
    ways = [c_bits + z_bits + x_bits + y_bits]
    for part in range(1, parts):
        ways.append(c_bits + (x_bits + y_bits if part % 2 else y_bits + x_bits) + z_bits)
    steps = len(ways[0])
    size = acc.shape[1]
    starts = [[0] for _ in range(parts)]
    at_step = [None] * parts
    flying = {}

    def partner(bit):
        axis, weight = bit
        mine = lax.rem(lax.div(index[axis], weight), 2)
        moved = dict(index)
        moved[axis] = index[axis] + (1 - 2 * mine) * weight
        return mine, moved["row"], moved["col"]

    def rows_at(start, length):
        return pl.ds(pl.multiple_of(start, 8), length)

    def landing(step):
        return size - (size >> step)

    def halve(part, step):
        half = size >> (step + 1)
        mine, to_row, to_col = partner(ways[part][step])
        start = starts[part][step]
        flying[part, step] = launch(
            acc.at[part, rows_at(start + (1 - mine) * half, half)],
            landed.at[part, pl.ds(landing(step), half)],
            s_send.at[part, step], s_recv.at[part, step], to_row, to_col,
        )
        starts[part].append(start + mine * half)

    def add(part, step):
        half = size >> (step + 1)
        start = starts[part][step + 1]
        target = gathered if step == steps - 1 else acc
        chunk = min(half, 256)

        def body(turn, carry):
            where = rows_at(start + turn * chunk, chunk)
            target[part, where, :] = (
                acc[part, where, :]
                + landed[part, rows_at(landing(step) + turn * chunk, chunk), :]
            )
            return carry

        lax.fori_loop(0, half // chunk, body, 0)

    def double(part, step):
        length = size >> (step + 1)
        _, to_row, to_col = partner(ways[part][step])
        where = rows_at(starts[part][step + 1], length)
        launch(
            gathered.at[part, where], gathered.at[part, where],
            g_send.at[part, step], g_recv.at[part, step], to_row, to_col,
        )

    def begin(part):
        if merged:
            at_step[part] = 0
            halve(part, 0)

    def advance(part):
        now = at_step[part]
        if now is None or now == 2 * steps:
            return
        at_step[part] = now + 1
        if now < steps:
            flying[part, now].wait_recv()
            add(part, now)
            if now + 1 < steps:
                halve(part, now + 1)
            else:
                double(part, now)
            return
        step = 2 * steps - 1 - now
        half = size >> (step + 1)
        mine, to_row, to_col = partner(ways[part][step])
        pltpu.make_async_remote_copy(
            src_ref=gathered.at[part, rows_at(starts[part][step + 1], half)],
            dst_ref=gathered.at[part, rows_at(starts[part][step] + (1 - mine) * half, half)],
            send_sem=g_send.at[part, step],
            recv_sem=g_recv.at[part, step],
            device_id=(to_row, to_col),
            device_id_type=pl.DeviceIdType.MESH,
        ).wait_recv()
        if step > 0:
            double(part, step - 1)

    def finish_node(node):
        column = -summed[node]
        if node > 0:
            column = column - times(summed[node - 1], links[node - 1], 1, 0)
        panels[node] = column.astype(panels.dtype)
        summed[node] = column
        if node == 0:
            padded(0, own, chosen_own)
        put(acc, first_of[node], times(own_rows(node), column, 0, 0))
        begin(first_of[node])
        if node + 1 < nodes:
            padded(node + 1, own, chosen_own)
            put(acc, first_of[node + 1] + 1, times(column, own_rows(node + 1), 0, 0))
            begin(first_of[node + 1] + 1)

    def own_rows(node):
        return dense[node, pl.ds(pl.multiple_of(place * panel_rows, 16), panel_rows), :]

    def last_steps(node):
        first = get(gathered, first_of[node], width)
        if node == 0:
            diags[0] = diags[0] - first
            return
        second = get(gathered, first_of[node] + 1, width)
        parents[node - 1] = -(second + times(diags[node - 1], links[node - 1], 1, 0))
        diags[node] = diags[node] - first - times(links[node - 1], parents[node - 1], 0, 0)

    start_z(0)
    deliver(0, 0)
    ancestor_copy = pltpu.make_async_copy(ancestor_given, ancestor, ancestor_sem)
    ancestor_copy.start()
    if merged:
        diag_copy = pltpu.make_async_copy(diag_inverse, diags, diag_sem)
        diag_copy.start()
    local = pltpu.make_async_copy(piece, own.at[:, here, :], local_sem)
    local.start()
    own_pending = []
    to_core = None

    def next_own():
        for copy in own_pending:
            copy.wait_recv()
        own_pending.clear()
        if len(own_slots) < row_count:
            own_pending.extend(own_step(bits_of(row_count).index(len(own_slots))))

    def turn_sums(turn):
        ended = []
        for earlier in range(min(turn, nodes)):
            level = turn - 1 - earlier
            if level < len(levels):
                end_sum(earlier, level)
                if level == len(levels) - 1:
                    ended.append(earlier)
        return ended

    def finish(ended):
        for node in ended:
            while own_pending or len(own_slots) < row_count:
                next_own()
            if node == 0:
                local.wait()
            finish_node(node)

    for node in range(nodes):
        for step in range(1, row_count):
            along_z[node, step].wait_recv()
            deliver(step, node)
            if step == 1 and node + 1 < nodes:
                start_z(node + 1)
                deliver(0, node + 1)
        next_own()
        arrive(node)
        padded(node, weights, chosen)
        if node == 0:
            ancestor_copy.wait()
        if to_core is not None:
            to_core.wait_send()
        given_core[...] = product(node, 1 - core)
        to_core = send(
            given_core, core_in.at[node], core_send.at[node], core_recv.at[node],
            row, col + 1 - 2 * core,
        )
        kept = product(node, core)
        for way in range(2):
            part = kept[:, :, way * half_width:(way + 1) * half_width]
            held[way][0][node] = part.reshape(view(way, mates) + part.shape[1:])
        ended = turn_sums(node)
        to_core.wait_recv()
        for way in range(2):
            part = core_in[node, :, :, halves[way]]
            held[way][0][node] += part.reshape(view(way, mates) + part.shape[1:])
            start_sum(node, way, 0)
        finish(ended)
    for turn in range(nodes, nodes + len(levels)):
        finish(turn_sums(turn))
        for part in range(parts):
            advance(part)
    to_core.wait_send()
    if merged:
        ended = 0
        diag_copy.wait()
        while ended < nodes:
            for part in range(parts):
                advance(part)
            while ended < nodes and all(
                at_step[part] == 2 * steps for part in range(first_of[ended] + (2 if ended else 1))
            ):
                last_steps(ended)
                ended += 1
    for target, remote in delivered:

        @pl.when(target != col)
        def _():
            remote.wait_send()

    for copy in waiting:
        copy.wait_send()


def marks(slot_tiles, block, tiles_per_block):
    ids = lax.dynamic_slice_in_dim(slot_tiles, block * CAP, CAP, 1) - block * tiles_per_block
    chosen = ids[:, :, None] == jnp.arange(tiles_per_block, dtype=ids.dtype)
    chosen = chosen.reshape(-1, CAP * tiles_per_block, 1).astype(jnp.float32)
    return jnp.broadcast_to(chosen, chosen.shape[:2] + (LANES,))


def run_kernel(
    merged, ancestor, factor_slots, slot_tiles, parent_factor, diag_inverse, row_count, col_count
):
    nodes, rows, width = factor_slots.shape
    block_rows, block_cols = ancestor.shape
    tiles_per_block = block_cols // TILE
    row, col = lax.axis_index("row"), lax.axis_index("col")
    own_block = row * (col_count // row_count) + col // row_count
    mates, panel_rows = col_count // 2, block_rows // col_count
    gathered = (nodes, row_count * rows, width)
    dma = pltpu.SemaphoreType.DMA
    levels = len(bits_of(col_count)) - 1
    vmem, f32, half_width = pltpu.VMEM, jnp.float32, width // 2
    tail = (panel_rows, half_width)
    low = [vmem((nodes, (mates >> j) // 2, 2) + tail, f32) for j in range(levels)]
    high = [vmem((nodes, 2, (mates >> j) // 2) + tail, f32) for j in range(levels)]
    came = [vmem((nodes, (mates >> j) // 2) + tail, f32) for j in range(levels)]
    parts, steps = 2 * nodes - 1, len(bits_of(row_count)) + len(bits_of(col_count))
    sums = (parts, width * width // LANES, LANES)
    out_shape = [jax.ShapeDtypeStruct((nodes, panel_rows, width), factor_slots.dtype)]
    extra = []
    if merged:
        out_shape += [
            jax.ShapeDtypeStruct((nodes, width, width), f32),
            jax.ShapeDtypeStruct((nodes - 1, width, width), f32),
        ]
        extra = [vmem(sums, f32)] * 3 + [dma((parts, steps))] * 4
    else:
        out_shape += [jax.ShapeDtypeStruct(sums, f32)]
    return pl.pallas_call(
        functools.partial(whole_kernel, row_count, col_count, merged),
        out_shape=out_shape,
        in_specs=[VMEM, VMEM, ANY, VMEM, VMEM, ANY],
        out_specs=[VMEM] * len(out_shape),
        scratch_shapes=extra + [
            vmem((mates, 2, panel_rows, block_cols), ancestor.dtype),
            dma,
            dma,
            vmem(gathered, factor_slots.dtype),
            vmem((nodes, panel_rows, width), f32),
            vmem(gathered, factor_slots.dtype),
            vmem((nodes, block_cols, width), factor_slots.dtype),
            vmem((row_count - 1, nodes, rows, width), factor_slots.dtype),
            vmem((mates, panel_rows, width), f32),
            vmem((nodes, mates, panel_rows, width), f32),
            dma((row_count - 1, nodes)),
            dma((row_count - 1, nodes)),
            dma((row_count, nodes)),
            dma((row_count, nodes)),
            dma((row_count - 1,)),
            dma((row_count - 1,)),
            dma,
            dma((nodes,)),
            dma((nodes,)),
            dma((nodes, 2, levels)),
            dma((nodes, 2, levels)),
        ] + low + high + came + came,
        compiler_params=pltpu.CompilerParams(
            collective_id=0, has_side_effects=True, vmem_limit_bytes=61 * 2**20
        ),
        name="selected_inverse",
    )(
        marks(slot_tiles, col, tiles_per_block),
        marks(slot_tiles, own_block, tiles_per_block),
        ancestor.reshape(mates, 2, panel_rows, block_cols),
        factor_slots, parent_factor, diag_inverse,
    )


def sum_kernel(orders, bounds, given, out, total, landed, rs_send, rs_recv, ag_send, ag_recv):
    index = {"row": lax.axis_index("row"), "col": lax.axis_index("col")}

    def partner(bit):
        axis, weight = bit
        mine = lax.rem(lax.div(index[axis], weight), 2)
        moved = dict(index)
        moved[axis] = index[axis] + (1 - 2 * mine) * weight
        return mine, moved["row"], moved["col"]

    greet([partner(bit)[1:] for bit in sorted(orders[0])])
    steps = len(orders[0])
    starts = [[base] for base, _ in bounds]
    copies = {}
    landing = [base for base, _ in bounds]

    def rows_at(start, length):
        return pl.ds(pl.multiple_of(start, 8), length)

    def halve(part, step):
        half = bounds[part][1] >> (step + 1)
        mine, row, col = partner(orders[part][step])
        start = starts[part][step]
        source = given if step == 0 else total
        copies[part, step] = send(
            source.at[rows_at(start + (1 - mine) * half, half)],
            landed.at[pl.ds(landing[part], half)],
            rs_send.at[part, step], rs_recv.at[part, step], row, col,
        )
        starts[part].append(start + mine * half)

    def add(part, step):
        half = bounds[part][1] >> (step + 1)
        start = starts[part][step + 1]
        source = given if step == 0 else total
        target = out if step == steps - 1 else total
        chunk = min(half, 32)

        def body(turn, carry):
            rows = rows_at(start + turn * chunk, chunk)
            target[rows, :] = (
                source[rows, :] + landed[rows_at(landing[part] + turn * chunk, chunk), :]
            )
            return carry

        lax.fori_loop(0, half // chunk, body, 0)
        landing[part] += half

    def double(part, step):
        length = bounds[part][1] >> (step + 1)
        _, row, col = partner(orders[part][step])
        where = rows_at(starts[part][step + 1], length)
        copies[part, steps + step] = send(
            out.at[where], out.at[where], ag_send.at[part, step], ag_recv.at[part, step], row, col
        )

    parts = range(len(orders))
    for part in parts:
        halve(part, 0)
    for step in range(steps):
        for part in parts:
            copies[part, step].wait_recv()
            add(part, step)
            if step + 1 < steps:
                halve(part, step + 1)
            else:
                double(part, step)
    for step in range(steps - 1, -1, -1):
        for part in parts:
            half = bounds[part][1] >> (step + 1)
            mine, row, col = partner(orders[part][step])
            pltpu.make_async_remote_copy(
                src_ref=out.at[rows_at(starts[part][step + 1], half)],
                dst_ref=out.at[rows_at(starts[part][step] + (1 - mine) * half, half)],
                send_sem=ag_send.at[part, step],
                recv_sem=ag_recv.at[part, step],
                device_id=(row, col),
                device_id_type=pl.DeviceIdType.MESH,
            ).wait_recv()
            if step > 0:
                double(part, step - 1)
    for copy in copies.values():
        copy.wait_send()


def sum_all(given, row_count, col_count):
    rows, width = given.shape
    col_bits, row_bits = bits_of(col_count), bits_of(row_count)
    half = 1 + (len(col_bits) - 1) // 2
    core = [("col", bit) for bit in col_bits[:1]]
    x = [("col", bit) for bit in col_bits[1:half]]
    y = [("col", bit) for bit in col_bits[half:]]
    z = [("row", bit) for bit in row_bits]
    orders = (core + x + y + z, core + y + x + z, core + z + x + y)
    unit = 8 * row_count * col_count
    units = max(3, -(-rows // unit))
    shares = (-(-units * 2 // 5), -(-units * 2 // 5))
    if units < 5:
        shares = (1, 1)
    shares = shares + (units - sum(shares),)
    bounds, base = [], 0
    for share in shares:
        bounds.append((base, share * unit))
        base += share * unit
    if base > rows:
        given = jnp.concatenate([given, jnp.zeros((base - rows, width), given.dtype)])
    shape = (base, width)
    dma = pltpu.SemaphoreType.DMA((len(orders), len(orders[0])))
    out = pl.pallas_call(
        functools.partial(sum_kernel, orders, bounds),
        out_shape=jax.ShapeDtypeStruct(shape, given.dtype),
        in_specs=[VMEM],
        out_specs=VMEM,
        scratch_shapes=[
            pltpu.VMEM(shape, given.dtype),
            pltpu.VMEM(shape, given.dtype),
            dma, dma, dma, dma,
        ],
        compiler_params=pltpu.CompilerParams(
            collective_id=1, has_side_effects=True, vmem_limit_bytes=56 * 2**20
        ),
        name="sum_all",
    )(given)
    return out[:rows]


def on_device(ancestor_inverse, factor_slots, slot_tiles, parent_factor, diag_inverse):
    row_count = lax.axis_size("row")
    col_count = lax.axis_size("col")
    nodes, _, width = factor_slots.shape
    merged = ancestor_inverse.shape[0] * width <= MERGED_SIZE
    results = run_kernel(
        merged, ancestor_inverse, factor_slots, slot_tiles, parent_factor, diag_inverse,
        row_count, col_count,
    )
    if merged:
        return tuple(results)
    panels, sums = results
    sums = sums.reshape(2 * nodes - 1, -1, width, LANES).transpose(0, 2, 1, 3)
    totals = sum_all(sums.reshape(-1, width), row_count, col_count)
    totals = totals.reshape(-1, width, width)
    diagonals = [diag_inverse[0] - totals[0]]
    parents = []
    for node in range(1, nodes):
        link = parent_factor[node - 1].astype(jnp.float32)
        upper = -(
            totals[2 * node] + jnp.dot(diagonals[-1], link, precision=exact_mode)
        )
        parents.append(upper)
        diagonals.append(
            diag_inverse[node] - totals[2 * node - 1]
            - jnp.dot(link.T, upper, precision=exact_mode)
        )
    return panels, jnp.stack(diagonals), jnp.stack(parents)


def solution(mesh):
    placed = (P("row", "col"), P(None, ("row", "col"), None), P(), P(), P())
    return jax.shard_map(
        on_device,
        mesh=mesh,
        in_specs=placed,
        out_specs=(P(None, ("row", "col"), None), P(), P()),
        check_vma=False,
    )
```

```python
import functools

import jax
import jax.numpy as jnp
from jax import lax
from jax.experimental import pallas as pl
from jax.experimental.pallas import tpu as pltpu
from jax.sharding import PartitionSpec as P

TILE = 256
CAP = 2
MERGED_SIZE = 1536 * 512


exact_mode = lax.Precision.HIGHEST


VMEM = pl.BlockSpec(memory_space=pltpu.VMEM)
ANY = pl.BlockSpec(memory_space=pl.ANY)


def send(src, dst, send_sem, recv_sem, row, col):
    copy = pltpu.make_async_remote_copy(
        src_ref=src,
        dst_ref=dst,
        send_sem=send_sem,
        recv_sem=recv_sem,
        device_id=(row, col),
        device_id_type=pl.DeviceIdType.MESH,
    )
    copy.start()
    return copy


def greet(peers):
    barrier = pltpu.get_barrier_semaphore()
    for row, col in peers:
        pl.semaphore_signal(
            barrier, inc=1, device_id=(row, col), device_id_type=pl.DeviceIdType.MESH
        )
    pl.semaphore_wait(barrier, len(peers))


def bits_of(count):
    return [1 << place for place in range(count.bit_length() - 1)]


def flipped(place, mask, bits):
    for bit in bits:
        if mask & bit:
            place = place + (1 - 2 * lax.rem(lax.div(place, bit), 2)) * bit
    return place


def split(value):
    parts = []
    for _ in range(3):
        part = value.astype(jnp.bfloat16)
        parts.append(part)
        value = value - part.astype(jnp.float32)
    return parts


def times(left, right, left_dim, right_dim):
    total = None
    lefts = split(left) if left.dtype == jnp.float32 else [left]
    rights = split(right) if right.dtype == jnp.float32 else [right]
    for one in lefts:
        for other in rights:
            term = lax.dot_general(
                one, other, (((left_dim,), (right_dim,)), ((), ())),
                preferred_element_type=jnp.float32,
            )
            total = term if total is None else total + term
    return total


LANES = 128


def put(ref, part, value):
    rows, width = value.shape
    for turn in range(width // LANES):
        ref[part, pl.ds(turn * rows, rows), :] = value[:, turn * LANES:(turn + 1) * LANES]


def get(ref, part, width):
    rows = ref.shape[1] * LANES // width
    return jnp.concatenate(
        [ref[part, pl.ds(turn * rows, rows), :] for turn in range(width // LANES)], axis=1
    )


def whole_kernel(row_count, col_count, merged, *refs):
    marked, ancestor_given, piece, links, diag_inverse, panels = refs[:6]
    chosen, chosen_own = marked.at[0], marked.at[1]
    if merged:
        diags, parents, acc, landed, gathered, s_send, s_recv, g_send, g_recv = refs[6:15]
        ancestor, ancestor_sem, diag_sem, own, summed, *scratch = refs[15:]
    else:
        acc = refs[6]
        ancestor, ancestor_sem, diag_sem, own, summed, *scratch = refs[7:]
    (weights, dense, passed, given_core, core_in, z_send, z_recv, w_send, w_recv, own_send, own_recv,
     local_sem, core_send, core_recv, rs_send, rs_recv) = scratch[:16]
    levels = bits_of(col_count)[1:]
    held = [scratch[16:16 + len(levels)], scratch[16 + len(levels):16 + 2 * len(levels)]]
    rest = scratch[16 + 2 * len(levels):]
    came = [rest[:len(levels)], rest[len(levels):]]
    orders = [levels, levels[::-1]]
    row, col = lax.axis_index("row"), lax.axis_index("col")
    groups = col_count // row_count
    nodes, rows, width = piece.shape
    half_width = width // 2
    place, group = lax.rem(col, row_count), lax.div(col, row_count)
    core = lax.rem(col, 2)
    mates, panel_rows = ancestor.shape[0], ancestor.shape[2]
    slot_rows = TILE
    tiles_per_block = ancestor.shape[3] // slot_rows
    greet(
        [(lax.rem(row + step, row_count), col) for step in range(1, row_count)]
        + [(row, lax.rem(col + step, col_count)) for step in range(1, col_count)]
    )
    here = pl.ds(pl.multiple_of(place * rows, rows), rows)
    waiting = []

    def launch(*arguments):
        copy = send(*arguments)
        waiting.append(copy)
        return copy

    along_z = {}

    def start_z(node):
        for step in range(1, row_count):
            along_z[node, step] = launch(
                piece.at[node], passed.at[step - 1, node],
                z_send.at[step - 1, node], z_recv.at[step - 1, node],
                lax.rem(row + step, row_count), col,
            )

    delivered = []

    def deliver(step, node):
        source = piece.at[node] if step == 0 else passed.at[step - 1, node]
        target = lax.rem(row - step + row_count, row_count) * groups + group
        remote = pltpu.make_async_remote_copy(
            src_ref=source,
            dst_ref=weights.at[node, here, :],
            send_sem=w_send.at[step, node],
            recv_sem=w_recv.at[place, node],
            device_id=(row, target),
            device_id_type=pl.DeviceIdType.MESH,
        )
        local = pltpu.make_async_copy(source, weights.at[node, here, :], w_send.at[step, node])

        @pl.when(target != col)
        def _():
            remote.start()

        @pl.when(target == col)
        def _():
            local.start()
            local.wait()

        delivered.append((target, remote))

    def arrive(node):
        for slot in range(row_count):
            origin = lax.rem(col, groups) * row_count + slot

            @pl.when(origin != col)
            def _():
                pltpu.make_async_remote_copy(
                    src_ref=piece.at[node],
                    dst_ref=weights.at[node, pl.ds(slot * rows, rows), :],
                    send_sem=w_send.at[0, node],
                    recv_sem=w_recv.at[slot, node],
                    device_id=(row, origin),
                    device_id_type=pl.DeviceIdType.MESH,
                ).wait_recv()

    def padded(node, slots_ref, marks):
        slots = [
            slots_ref[node, pl.ds(member * slot_rows, slot_rows), :].astype(jnp.float32)
            for member in range(CAP)
        ]
        lines = [
            jnp.concatenate([marks[node, pl.ds(line, 1), :]] * (width // LANES), axis=1)
            for line in range(CAP * tiles_per_block)
        ]
        for tile in range(tiles_per_block):
            total = None
            for member in range(CAP):
                line = member * tiles_per_block + tile
                term = slots[member] * lines[line]
                total = term if total is None else total + term
            dense[node, pl.ds(tile * slot_rows, slot_rows), :] = total.astype(dense.dtype)

    def product(node, side):
        block = ancestor[:, side, :, :].reshape(mates * panel_rows, ancestor.shape[3])
        total = jnp.dot(block, dense[node], preferred_element_type=jnp.float32)
        return total.reshape(mates, panel_rows, width)

    halves = [pl.ds(0, half_width), pl.ds(half_width, half_width)]

    def view(way, length):
        return (length // 2, 2) if way == 0 else (2, length // 2)

    def at_bit(way, node, value):
        return (node, slice(None), value) if way == 0 else (node, value)

    sums = {}

    def start_sum(node, way, level):
        bit = orders[way][level]
        mine = lax.rem(lax.div(col, bit), 2)
        sums[node, way, level] = launch(
            held[way][level].at[at_bit(way, node, 1 - mine)], came[way][level].at[node],
            rs_send.at[node, way, level], rs_recv.at[node, way, level],
            row, col + (1 - 2 * mine) * bit,
        )

    def end_sum(node, level):
        for way in range(2):
            mine = lax.rem(lax.div(col, orders[way][level]), 2)
            sums[node, way, level].wait_recv()
            value = held[way][level][at_bit(way, node, mine)] + came[way][level][node]
            length = value.shape[0]
            if level + 1 < len(levels):
                held[way][level + 1][node] = value.reshape(view(way, length) + value.shape[1:])
                start_sum(node, way, level + 1)
            else:
                summed[node, :, halves[way]] = value[0]

    own_slots = [0]
    own_steps = bits_of(row_count)[::-1]

    def own_step(number):
        bit = own_steps[number]
        base = len(own_slots) - 1
        copies = []
        for offset, mask in enumerate(own_slots):
            slot = flipped(place, mask, own_steps)
            where = pl.ds(pl.multiple_of(slot * rows, rows), rows)
            target = group * row_count + flipped(place, bit, own_steps)
            copies.append(
                launch(
                    piece if mask == 0 else own.at[:, where, :], own.at[:, where, :],
                    own_send.at[base + offset], own_recv.at[base + offset], row, target,
                )
            )
        own_slots.extend([mask ^ bit for mask in own_slots])
        return copies

    parts = 2 * nodes - 1
    first_of = [0] + [2 * node - 1 for node in range(1, nodes)]
    index = {"row": row, "col": col}
    col_bits, row_bits = bits_of(col_count), bits_of(row_count)
    middle = 1 + (len(col_bits) - 1) // 2
    c_bits = [("col", bit) for bit in col_bits[:1]]
    x_bits = [("col", bit) for bit in col_bits[1:middle]]
    y_bits = [("col", bit) for bit in col_bits[middle:]]
    z_bits = [("row", bit) for bit in row_bits]
    ways = [c_bits + z_bits + x_bits + y_bits]
    for part in range(1, parts):
        plane = x_bits + y_bits if part % 2 else y_bits + x_bits
        ways.append(c_bits + (z_bits + plane if part == 2 else plane + z_bits))
    steps = len(ways[0])
    size = acc.shape[1]
    starts = [[0] for _ in range(parts)]
    at_step = [None] * parts
    flying = {}

    def partner(bit):
        axis, weight = bit
        mine = lax.rem(lax.div(index[axis], weight), 2)
        moved = dict(index)
        moved[axis] = index[axis] + (1 - 2 * mine) * weight
        return mine, moved["row"], moved["col"]

    def rows_at(start, length):
        return pl.ds(pl.multiple_of(start, 8), length)

    def landing(step):
        return size - (size >> step)

    def halve(part, step):
        half = size >> (step + 1)
        mine, to_row, to_col = partner(ways[part][step])
        start = starts[part][step]
        flying[part, step] = launch(
            acc.at[part, rows_at(start + (1 - mine) * half, half)],
            landed.at[part, pl.ds(landing(step), half)],
            s_send.at[part, step], s_recv.at[part, step], to_row, to_col,
        )
        starts[part].append(start + mine * half)

    def add(part, step):
        half = size >> (step + 1)
        start = starts[part][step + 1]
        target = gathered if step == steps - 1 else acc
        chunk = min(half, 256)

        def body(turn, carry):
            where = rows_at(start + turn * chunk, chunk)
            target[part, where, :] = (
                acc[part, where, :]
                + landed[part, rows_at(landing(step) + turn * chunk, chunk), :]
            )
            return carry

        lax.fori_loop(0, half // chunk, body, 0)

    def double(part, step):
        length = size >> (step + 1)
        _, to_row, to_col = partner(ways[part][step])
        where = rows_at(starts[part][step + 1], length)
        launch(
            gathered.at[part, where], gathered.at[part, where],
            g_send.at[part, step], g_recv.at[part, step], to_row, to_col,
        )

    def begin(part):
        if merged:
            at_step[part] = 0
            halve(part, 0)

    def advance(part):
        now = at_step[part]
        if now is None or now == 2 * steps:
            return
        at_step[part] = now + 1
        if now < steps:
            flying[part, now].wait_recv()
            add(part, now)
            if now + 1 < steps:
                halve(part, now + 1)
            else:
                double(part, now)
            return
        step = 2 * steps - 1 - now
        half = size >> (step + 1)
        mine, to_row, to_col = partner(ways[part][step])
        pltpu.make_async_remote_copy(
            src_ref=gathered.at[part, rows_at(starts[part][step + 1], half)],
            dst_ref=gathered.at[part, rows_at(starts[part][step] + (1 - mine) * half, half)],
            send_sem=g_send.at[part, step],
            recv_sem=g_recv.at[part, step],
            device_id=(to_row, to_col),
            device_id_type=pl.DeviceIdType.MESH,
        ).wait_recv()
        if step > 0:
            double(part, step - 1)

    def finish_node(node):
        column = -summed[node]
        if node > 0:
            column = column - times(summed[node - 1], links[node - 1], 1, 0)
        panels[node] = column.astype(panels.dtype)
        summed[node] = column
        if node == 0:
            padded(0, own, chosen_own)
        put(acc, first_of[node], times(own_rows(node), column, 0, 0))
        begin(first_of[node])
        if node + 1 < nodes:
            padded(node + 1, own, chosen_own)
            put(acc, first_of[node + 1] + 1, times(column, own_rows(node + 1), 0, 0))
            begin(first_of[node + 1] + 1)

    def own_rows(node):
        return dense[node, pl.ds(pl.multiple_of(place * panel_rows, 16), panel_rows), :]

    def last_steps(node):
        first = get(gathered, first_of[node], width)
        if node == 0:
            diags[0] = diags[0] - first
            parents[0] = times(diags[0], links[0], 1, 0)
            return
        second = get(gathered, first_of[node] + 1, width)
        parents[node - 1] = -(second + parents[node - 1])
        diags[node] = diags[node] - first - times(links[node - 1], parents[node - 1], 0, 0)
        if node + 1 < nodes:
            parents[node] = times(diags[node], links[node], 1, 0)

    start_z(0)
    deliver(0, 0)
    ancestor_copy = pltpu.make_async_copy(ancestor_given, ancestor, ancestor_sem)
    ancestor_copy.start()
    if merged:
        diag_copy = pltpu.make_async_copy(diag_inverse, diags, diag_sem)
        diag_copy.start()
    local = pltpu.make_async_copy(piece, own.at[:, here, :], local_sem)
    local.start()
    own_pending = []
    to_core = None

    def next_own():
        for copy in own_pending:
            copy.wait_recv()
        own_pending.clear()
        if len(own_slots) < row_count:
            own_pending.extend(own_step(bits_of(row_count).index(len(own_slots))))

    def turn_sums(turn):
        ended = []
        for earlier in range(min(turn, nodes)):
            level = turn - 1 - earlier
            if level < len(levels):
                end_sum(earlier, level)
                if level == len(levels) - 1:
                    ended.append(earlier)
        return ended

    def finish(ended):
        for node in ended:
            while own_pending or len(own_slots) < row_count:
                next_own()
            if node == 0:
                local.wait()
            finish_node(node)

    for node in range(nodes):
        for step in range(1, row_count):
            along_z[node, step].wait_recv()
            deliver(step, node)
            if step == 1 and node + 1 < nodes:
                start_z(node + 1)
                deliver(0, node + 1)
        next_own()
        arrive(node)
        padded(node, weights, chosen)
        if node == 0:
            ancestor_copy.wait()
        if to_core is not None:
            to_core.wait_send()
        given_core[...] = product(node, 1 - core)
        to_core = send(
            given_core, core_in.at[node], core_send.at[node], core_recv.at[node],
            row, col + 1 - 2 * core,
        )
        kept = product(node, core)
        for way in range(2):
            part = kept[:, :, way * half_width:(way + 1) * half_width]
            held[way][0][node] = part.reshape(view(way, mates) + part.shape[1:])
        ended = turn_sums(node)
        to_core.wait_recv()
        for way in range(2):
            part = core_in[node, :, :, halves[way]]
            held[way][0][node] += part.reshape(view(way, mates) + part.shape[1:])
            start_sum(node, way, 0)
        finish(ended)
    for turn in range(nodes, nodes + len(levels)):
        finish(turn_sums(turn))
        for part in range(parts):
            advance(part)
    to_core.wait_send()
    if merged:
        ended = 0
        diag_copy.wait()
        while ended < nodes:
            for part in range(parts):
                advance(part)
            while ended < nodes and all(
                at_step[part] == 2 * steps for part in range(first_of[ended] + (2 if ended else 1))
            ):
                last_steps(ended)
                ended += 1
    for target, remote in delivered:

        @pl.when(target != col)
        def _():
            remote.wait_send()

    for copy in waiting:
        copy.wait_send()


def marks(slot_tiles, blocks, tiles_per_block):
    nodes, slots = slot_tiles.shape
    count = slots // CAP
    shape = (len(blocks), nodes, CAP, tiles_per_block, LANES, count)
    wanted = jnp.stack(blocks).astype(jnp.int32)[:, None, None, None, None, None]
    block = lax.broadcasted_iota(jnp.int32, shape, 5)
    tile = block * tiles_per_block + lax.broadcasted_iota(jnp.int32, shape, 3)
    ids = slot_tiles.reshape(nodes, count, CAP).transpose(0, 2, 1)[None, :, :, None, None, :]
    hits = (ids == tile) & (block == wanted)
    chosen = jnp.sum(jnp.where(hits, 1.0, 0.0).astype(jnp.float32), axis=5)
    return chosen.reshape(len(blocks), nodes, CAP * tiles_per_block, LANES)


def run_kernel(
    merged, ancestor, factor_slots, slot_tiles, parent_factor, diag_inverse, row_count, col_count
):
    nodes, rows, width = factor_slots.shape
    block_rows, block_cols = ancestor.shape
    tiles_per_block = block_cols // TILE
    row, col = lax.axis_index("row"), lax.axis_index("col")
    own_block = row * (col_count // row_count) + col // row_count
    mates, panel_rows = col_count // 2, block_rows // col_count
    gathered = (nodes, row_count * rows, width)
    dma = pltpu.SemaphoreType.DMA
    levels = len(bits_of(col_count)) - 1
    vmem, f32, half_width = pltpu.VMEM, jnp.float32, width // 2
    tail = (panel_rows, half_width)
    low = [vmem((nodes, (mates >> j) // 2, 2) + tail, f32) for j in range(levels)]
    high = [vmem((nodes, 2, (mates >> j) // 2) + tail, f32) for j in range(levels)]
    came = [vmem((nodes, (mates >> j) // 2) + tail, f32) for j in range(levels)]
    parts, steps = 2 * nodes - 1, len(bits_of(row_count)) + len(bits_of(col_count))
    sums = (parts, width * width // LANES, LANES)
    out_shape = [jax.ShapeDtypeStruct((nodes, panel_rows, width), factor_slots.dtype)]
    extra = []
    if merged:
        out_shape += [
            jax.ShapeDtypeStruct((nodes, width, width), f32),
            jax.ShapeDtypeStruct((nodes - 1, width, width), f32),
        ]
        extra = [vmem(sums, f32)] * 3 + [dma((parts, steps))] * 4
    else:
        out_shape += [jax.ShapeDtypeStruct(sums, f32)]
    return pl.pallas_call(
        functools.partial(whole_kernel, row_count, col_count, merged),
        out_shape=out_shape,
        in_specs=[VMEM, ANY, VMEM, VMEM, ANY],
        out_specs=[VMEM] * len(out_shape),
        scratch_shapes=extra + [
            vmem((mates, 2, panel_rows, block_cols), ancestor.dtype),
            dma,
            dma,
            vmem(gathered, factor_slots.dtype),
            vmem((nodes, panel_rows, width), f32),
            vmem(gathered, factor_slots.dtype),
            vmem((nodes, block_cols, width), factor_slots.dtype),
            vmem((row_count - 1, nodes, rows, width), factor_slots.dtype),
            vmem((mates, panel_rows, width), f32),
            vmem((nodes, mates, panel_rows, width), f32),
            dma((row_count - 1, nodes)),
            dma((row_count - 1, nodes)),
            dma((row_count, nodes)),
            dma((row_count, nodes)),
            dma((row_count - 1,)),
            dma((row_count - 1,)),
            dma,
            dma((nodes,)),
            dma((nodes,)),
            dma((nodes, 2, levels)),
            dma((nodes, 2, levels)),
        ] + low + high + came + came,
        compiler_params=pltpu.CompilerParams(
            collective_id=0, has_side_effects=True, vmem_limit_bytes=61 * 2**20
        ),
        name="selected_inverse",
    )(
        marks(slot_tiles, (col, own_block), tiles_per_block),
        ancestor.reshape(mates, 2, panel_rows, block_cols),
        factor_slots, parent_factor, diag_inverse,
    )


def sum_kernel(orders, bounds, given, out, total, landed, rs_send, rs_recv, ag_send, ag_recv):
    index = {"row": lax.axis_index("row"), "col": lax.axis_index("col")}

    def partner(bit):
        axis, weight = bit
        mine = lax.rem(lax.div(index[axis], weight), 2)
        moved = dict(index)
        moved[axis] = index[axis] + (1 - 2 * mine) * weight
        return mine, moved["row"], moved["col"]

    greet([partner(bit)[1:] for bit in sorted(orders[0])])
    steps = len(orders[0])
    starts = [[base] for base, _ in bounds]
    copies = {}
    landing = [base for base, _ in bounds]

    def rows_at(start, length):
        return pl.ds(pl.multiple_of(start, 8), length)

    def halve(part, step):
        half = bounds[part][1] >> (step + 1)
        mine, row, col = partner(orders[part][step])
        start = starts[part][step]
        source = given if step == 0 else total
        copies[part, step] = send(
            source.at[rows_at(start + (1 - mine) * half, half)],
            landed.at[pl.ds(landing[part], half)],
            rs_send.at[part, step], rs_recv.at[part, step], row, col,
        )
        starts[part].append(start + mine * half)

    def add(part, step):
        half = bounds[part][1] >> (step + 1)
        start = starts[part][step + 1]
        source = given if step == 0 else total
        target = out if step == steps - 1 else total
        chunk = min(half, 32)

        def body(turn, carry):
            rows = rows_at(start + turn * chunk, chunk)
            target[rows, :] = (
                source[rows, :] + landed[rows_at(landing[part] + turn * chunk, chunk), :]
            )
            return carry

        lax.fori_loop(0, half // chunk, body, 0)
        landing[part] += half

    def double(part, step):
        length = bounds[part][1] >> (step + 1)
        _, row, col = partner(orders[part][step])
        where = rows_at(starts[part][step + 1], length)
        copies[part, steps + step] = send(
            out.at[where], out.at[where], ag_send.at[part, step], ag_recv.at[part, step], row, col
        )

    parts = range(len(orders))
    for part in parts:
        halve(part, 0)
    for step in range(steps):
        for part in parts:
            copies[part, step].wait_recv()
            add(part, step)
            if step + 1 < steps:
                halve(part, step + 1)
            else:
                double(part, step)
    for step in range(steps - 1, -1, -1):
        for part in parts:
            half = bounds[part][1] >> (step + 1)
            mine, row, col = partner(orders[part][step])
            pltpu.make_async_remote_copy(
                src_ref=out.at[rows_at(starts[part][step + 1], half)],
                dst_ref=out.at[rows_at(starts[part][step] + (1 - mine) * half, half)],
                send_sem=ag_send.at[part, step],
                recv_sem=ag_recv.at[part, step],
                device_id=(row, col),
                device_id_type=pl.DeviceIdType.MESH,
            ).wait_recv()
            if step > 0:
                double(part, step - 1)
    for copy in copies.values():
        copy.wait_send()


def sum_all(given, row_count, col_count):
    rows, width = given.shape
    col_bits, row_bits = bits_of(col_count), bits_of(row_count)
    half = 1 + (len(col_bits) - 1) // 2
    core = [("col", bit) for bit in col_bits[:1]]
    x = [("col", bit) for bit in col_bits[1:half]]
    y = [("col", bit) for bit in col_bits[half:]]
    z = [("row", bit) for bit in row_bits]
    orders = (core + x + y + z, core + y + x + z, core + z + x + y)
    unit = 8 * row_count * col_count
    units = max(3, -(-rows // unit))
    shares = (-(-units * 2 // 5), -(-units * 2 // 5))
    if units < 5:
        shares = (1, 1)
    shares = shares + (units - sum(shares),)
    bounds, base = [], 0
    for share in shares:
        bounds.append((base, share * unit))
        base += share * unit
    if base > rows:
        given = jnp.concatenate([given, jnp.zeros((base - rows, width), given.dtype)])
    shape = (base, width)
    dma = pltpu.SemaphoreType.DMA((len(orders), len(orders[0])))
    out = pl.pallas_call(
        functools.partial(sum_kernel, orders, bounds),
        out_shape=jax.ShapeDtypeStruct(shape, given.dtype),
        in_specs=[VMEM],
        out_specs=VMEM,
        scratch_shapes=[
            pltpu.VMEM(shape, given.dtype),
            pltpu.VMEM(shape, given.dtype),
            dma, dma, dma, dma,
        ],
        compiler_params=pltpu.CompilerParams(
            collective_id=1, has_side_effects=True, vmem_limit_bytes=56 * 2**20
        ),
        name="sum_all",
    )(given)
    return out[:rows]


def on_device(ancestor_inverse, factor_slots, slot_tiles, parent_factor, diag_inverse):
    row_count = lax.axis_size("row")
    col_count = lax.axis_size("col")
    nodes, _, width = factor_slots.shape
    merged = ancestor_inverse.shape[0] * width <= MERGED_SIZE
    results = run_kernel(
        merged, ancestor_inverse, factor_slots, slot_tiles, parent_factor, diag_inverse,
        row_count, col_count,
    )
    if merged:
        return tuple(results)
    panels, sums = results
    sums = sums.reshape(2 * nodes - 1, -1, width, LANES).transpose(0, 2, 1, 3)
    totals = sum_all(sums.reshape(-1, width), row_count, col_count)
    totals = totals.reshape(-1, width, width)
    diagonals = [diag_inverse[0] - totals[0]]
    parents = []
    for node in range(1, nodes):
        link = parent_factor[node - 1].astype(jnp.float32)
        upper = -(
            totals[2 * node] + jnp.dot(diagonals[-1], link, precision=exact_mode)
        )
        parents.append(upper)
        diagonals.append(
            diag_inverse[node] - totals[2 * node - 1]
            - jnp.dot(link.T, upper, precision=exact_mode)
        )
    return panels, jnp.stack(diagonals), jnp.stack(parents)


def solution(mesh):
    placed = (P("row", "col"), P(None, ("row", "col"), None), P(), P(), P())
    return jax.shard_map(
        on_device,
        mesh=mesh,
        in_specs=placed,
        out_specs=(P(None, ("row", "col"), None), P(), P()),
        check_vma=False,
    )
```

```python
import functools

import jax
import jax.numpy as jnp
from jax import lax
from jax.experimental import pallas as pl
from jax.experimental.pallas import tpu as pltpu
from jax.sharding import PartitionSpec as P

TILE = 256
CAP = 2
MERGED_SIZE = 1536 * 512


exact_mode = lax.Precision.HIGHEST


VMEM = pl.BlockSpec(memory_space=pltpu.VMEM)
ANY = pl.BlockSpec(memory_space=pl.ANY)


def send(src, dst, send_sem, recv_sem, row, col):
    copy = pltpu.make_async_remote_copy(
        src_ref=src,
        dst_ref=dst,
        send_sem=send_sem,
        recv_sem=recv_sem,
        device_id=(row, col),
        device_id_type=pl.DeviceIdType.MESH,
    )
    copy.start()
    return copy


def greet(peers):
    barrier = pltpu.get_barrier_semaphore()
    for row, col in peers:
        pl.semaphore_signal(
            barrier, inc=1, device_id=(row, col), device_id_type=pl.DeviceIdType.MESH
        )
    pl.semaphore_wait(barrier, len(peers))


def bits_of(count):
    return [1 << place for place in range(count.bit_length() - 1)]


def flipped(place, mask, bits):
    for bit in bits:
        if mask & bit:
            place = place + (1 - 2 * lax.rem(lax.div(place, bit), 2)) * bit
    return place


def split(value):
    parts = []
    for _ in range(3):
        part = value.astype(jnp.bfloat16)
        parts.append(part)
        value = value - part.astype(jnp.float32)
    return parts


def times(left, right, left_dim, right_dim):
    total = None
    lefts = split(left) if left.dtype == jnp.float32 else [left]
    rights = split(right) if right.dtype == jnp.float32 else [right]
    for one in lefts:
        for other in rights:
            term = lax.dot_general(
                one, other, (((left_dim,), (right_dim,)), ((), ())),
                preferred_element_type=jnp.float32,
            )
            total = term if total is None else total + term
    return total


LANES = 128


def put(ref, part, value):
    rows, width = value.shape
    for turn in range(width // LANES):
        ref[part, pl.ds(turn * rows, rows), :] = value[:, turn * LANES:(turn + 1) * LANES]


def get(ref, part, width):
    rows = ref.shape[1] * LANES // width
    return jnp.concatenate(
        [ref[part, pl.ds(turn * rows, rows), :] for turn in range(width // LANES)], axis=1
    )


def whole_kernel(row_count, col_count, merged, *refs):
    marked, ancestor_given, piece, links, diag_inverse, panels = refs[:6]
    chosen, chosen_own = marked.at[0], marked.at[1]
    if merged:
        diags, parents, acc, landed, gathered, s_send, s_recv, g_send, g_recv = refs[6:15]
        ancestor, ancestor_sem, diag_sem, own, summed, *scratch = refs[15:]
    else:
        acc = refs[6]
        ancestor, ancestor_sem, diag_sem, own, summed, *scratch = refs[7:]
    (weights, dense, passed, given_core, core_in, z_send, z_recv, w_send, w_recv, own_send, own_recv,
     local_sem, core_send, core_recv, rs_send, rs_recv) = scratch[:16]
    levels = bits_of(col_count)[1:]
    held = [scratch[16:16 + len(levels)], scratch[16 + len(levels):16 + 2 * len(levels)]]
    rest = scratch[16 + 2 * len(levels):]
    came = [rest[:len(levels)], rest[len(levels):]]
    orders = [levels, levels[::-1]]
    row, col = lax.axis_index("row"), lax.axis_index("col")
    groups = col_count // row_count
    nodes, rows, width = piece.shape
    half_width = width // 2
    place, group = lax.rem(col, row_count), lax.div(col, row_count)
    core = lax.rem(col, 2)
    mates, panel_rows = ancestor.shape[0], ancestor.shape[2]
    slot_rows = TILE
    tiles_per_block = ancestor.shape[3] // slot_rows
    greet(
        [(lax.rem(row + step, row_count), col) for step in range(1, row_count)]
        + [(row, lax.rem(col + step, col_count)) for step in range(1, col_count)]
    )
    here = pl.ds(pl.multiple_of(place * rows, rows), rows)
    waiting = []

    def launch(*arguments):
        copy = send(*arguments)
        waiting.append(copy)
        return copy

    along_z = {}

    def start_z(node):
        for step in range(1, row_count):
            along_z[node, step] = launch(
                piece.at[node], passed.at[step - 1, node],
                z_send.at[step - 1, node], z_recv.at[step - 1, node],
                lax.rem(row + step, row_count), col,
            )

    delivered = []

    def deliver(step, node):
        source = piece.at[node] if step == 0 else passed.at[step - 1, node]
        target = lax.rem(row - step + row_count, row_count) * groups + group
        remote = pltpu.make_async_remote_copy(
            src_ref=source,
            dst_ref=weights.at[node, here, :],
            send_sem=w_send.at[step, node],
            recv_sem=w_recv.at[place, node],
            device_id=(row, target),
            device_id_type=pl.DeviceIdType.MESH,
        )
        local = pltpu.make_async_copy(source, weights.at[node, here, :], w_send.at[step, node])

        @pl.when(target != col)
        def _():
            remote.start()

        @pl.when(target == col)
        def _():
            local.start()
            local.wait()

        delivered.append((target, remote))

    def arrive(node):
        for slot in range(row_count):
            origin = lax.rem(col, groups) * row_count + slot

            @pl.when(origin != col)
            def _():
                pltpu.make_async_remote_copy(
                    src_ref=piece.at[node],
                    dst_ref=weights.at[node, pl.ds(slot * rows, rows), :],
                    send_sem=w_send.at[0, node],
                    recv_sem=w_recv.at[slot, node],
                    device_id=(row, origin),
                    device_id_type=pl.DeviceIdType.MESH,
                ).wait_recv()

    def padded(node, slots_ref, marks):
        slots = [
            slots_ref[node, pl.ds(member * slot_rows, slot_rows), :].astype(jnp.float32)
            for member in range(CAP)
        ]
        lines = [
            jnp.concatenate([marks[node, pl.ds(line, 1), :]] * (width // LANES), axis=1)
            for line in range(CAP * tiles_per_block)
        ]
        for tile in range(tiles_per_block):
            total = None
            for member in range(CAP):
                line = member * tiles_per_block + tile
                term = slots[member] * lines[line]
                total = term if total is None else total + term
            dense[node, pl.ds(tile * slot_rows, slot_rows), :] = total.astype(dense.dtype)

    def product(node, side):
        block = ancestor[:, side, :, :].reshape(mates * panel_rows, ancestor.shape[3])
        total = jnp.dot(block, dense[node], preferred_element_type=jnp.float32)
        return total.reshape(mates, panel_rows, width)

    halves = [pl.ds(0, half_width), pl.ds(half_width, half_width)]

    def view(way, length):
        return (length // 2, 2) if way == 0 else (2, length // 2)

    def at_bit(way, node, value):
        return (node, slice(None), value) if way == 0 else (node, value)

    sums = {}

    def start_sum(node, way, level):
        bit = orders[way][level]
        mine = lax.rem(lax.div(col, bit), 2)
        sums[node, way, level] = launch(
            held[way][level].at[at_bit(way, node, 1 - mine)], came[way][level].at[node],
            rs_send.at[node, way, level], rs_recv.at[node, way, level],
            row, col + (1 - 2 * mine) * bit,
        )

    def end_sum(node, level):
        for way in range(2):
            mine = lax.rem(lax.div(col, orders[way][level]), 2)
            sums[node, way, level].wait_recv()
            value = held[way][level][at_bit(way, node, mine)] + came[way][level][node]
            length = value.shape[0]
            if level + 1 < len(levels):
                held[way][level + 1][node] = value.reshape(view(way, length) + value.shape[1:])
                start_sum(node, way, level + 1)
            else:
                summed[node, :, halves[way]] = value[0]

    own_slots = [0]
    own_steps = bits_of(row_count)[::-1]

    def own_step(number):
        bit = own_steps[number]
        base = len(own_slots) - 1
        copies = []
        for offset, mask in enumerate(own_slots):
            slot = flipped(place, mask, own_steps)
            where = pl.ds(pl.multiple_of(slot * rows, rows), rows)
            target = group * row_count + flipped(place, bit, own_steps)
            copies.append(
                launch(
                    piece if mask == 0 else own.at[:, where, :], own.at[:, where, :],
                    own_send.at[base + offset], own_recv.at[base + offset], row, target,
                )
            )
        own_slots.extend([mask ^ bit for mask in own_slots])
        return copies

    parts = 2 * nodes - 1
    first_of = [0] + [2 * node - 1 for node in range(1, nodes)]
    index = {"row": row, "col": col}
    col_bits, row_bits = bits_of(col_count), bits_of(row_count)
    middle = 1 + (len(col_bits) - 1) // 2
    c_bits = [("col", bit) for bit in col_bits[:1]]
    x_bits = [("col", bit) for bit in col_bits[1:middle]]
    y_bits = [("col", bit) for bit in col_bits[middle:]]
    z_bits = [("row", bit) for bit in row_bits]
    ways = [c_bits + z_bits + x_bits + y_bits]
    for part in range(1, parts):
        plane = x_bits + y_bits if part % 2 else y_bits + x_bits
        ways.append(c_bits + plane + z_bits)
    steps = len(ways[0])
    size = acc.shape[1]
    starts = [[0] for _ in range(parts)]
    at_step = [None] * parts
    flying = {}

    def partner(bit):
        axis, weight = bit
        mine = lax.rem(lax.div(index[axis], weight), 2)
        moved = dict(index)
        moved[axis] = index[axis] + (1 - 2 * mine) * weight
        return mine, moved["row"], moved["col"]

    def rows_at(start, length):
        return pl.ds(pl.multiple_of(start, 8), length)

    def landing(step):
        return size - (size >> step)

    def halve(part, step):
        half = size >> (step + 1)
        mine, to_row, to_col = partner(ways[part][step])
        start = starts[part][step]
        flying[part, step] = launch(
            acc.at[part, rows_at(start + (1 - mine) * half, half)],
            landed.at[part, pl.ds(landing(step), half)],
            s_send.at[part, step], s_recv.at[part, step], to_row, to_col,
        )
        starts[part].append(start + mine * half)

    def add(part, step):
        half = size >> (step + 1)
        start = starts[part][step + 1]
        target = gathered if step == steps - 1 else acc
        chunk = min(half, 256)

        def body(turn, carry):
            where = rows_at(start + turn * chunk, chunk)
            target[part, where, :] = (
                acc[part, where, :]
                + landed[part, rows_at(landing(step) + turn * chunk, chunk), :]
            )
            return carry

        lax.fori_loop(0, half // chunk, body, 0)

    def double(part, step):
        length = size >> (step + 1)
        _, to_row, to_col = partner(ways[part][step])
        where = rows_at(starts[part][step + 1], length)
        launch(
            gathered.at[part, where], gathered.at[part, where],
            g_send.at[part, step], g_recv.at[part, step], to_row, to_col,
        )

    def begin(part):
        if merged:
            at_step[part] = 0
            halve(part, 0)

    def advance(part):
        now = at_step[part]
        if now is None or now == 2 * steps:
            return
        at_step[part] = now + 1
        if now < steps:
            flying[part, now].wait_recv()
            add(part, now)
            if now + 1 < steps:
                halve(part, now + 1)
            else:
                double(part, now)
            return
        step = 2 * steps - 1 - now
        half = size >> (step + 1)
        mine, to_row, to_col = partner(ways[part][step])
        pltpu.make_async_remote_copy(
            src_ref=gathered.at[part, rows_at(starts[part][step + 1], half)],
            dst_ref=gathered.at[part, rows_at(starts[part][step] + (1 - mine) * half, half)],
            send_sem=g_send.at[part, step],
            recv_sem=g_recv.at[part, step],
            device_id=(to_row, to_col),
            device_id_type=pl.DeviceIdType.MESH,
        ).wait_recv()
        if step > 0:
            double(part, step - 1)

    def finish_node(node):
        column = -summed[node]
        if node > 0:
            column = column - times(summed[node - 1], links[node - 1], 1, 0)
        panels[node] = column.astype(panels.dtype)
        summed[node] = column
        if node == 0:
            padded(0, own, chosen_own)
        put(acc, first_of[node], times(own_rows(node), column, 0, 0))
        begin(first_of[node])
        if node + 1 < nodes:
            padded(node + 1, own, chosen_own)
            put(acc, first_of[node + 1] + 1, times(column, own_rows(node + 1), 0, 0))
            begin(first_of[node + 1] + 1)

    def own_rows(node):
        return dense[node, pl.ds(pl.multiple_of(place * panel_rows, 16), panel_rows), :]

    def last_steps(node):
        first = get(gathered, first_of[node], width)
        if node == 0:
            diags[0] = diags[0] - first
            parents[0] = times(diags[0], links[0], 1, 0)
            return
        second = get(gathered, first_of[node] + 1, width)
        parents[node - 1] = -(second + parents[node - 1])
        diags[node] = diags[node] - first - times(links[node - 1], parents[node - 1], 0, 0)
        if node + 1 < nodes:
            parents[node] = times(diags[node], links[node], 1, 0)

    start_z(0)
    deliver(0, 0)
    ancestor_copy = pltpu.make_async_copy(ancestor_given, ancestor, ancestor_sem)
    ancestor_copy.start()
    if merged:
        diag_copy = pltpu.make_async_copy(diag_inverse, diags, diag_sem)
        diag_copy.start()
    local = pltpu.make_async_copy(piece, own.at[:, here, :], local_sem)
    local.start()
    own_pending = []
    to_core = None

    def next_own():
        for copy in own_pending:
            copy.wait_recv()
        own_pending.clear()
        if len(own_slots) < row_count:
            own_pending.extend(own_step(bits_of(row_count).index(len(own_slots))))

    def turn_sums(turn):
        ended = []
        for earlier in range(min(turn, nodes)):
            level = turn - 1 - earlier
            if level < len(levels):
                end_sum(earlier, level)
                if level == len(levels) - 1:
                    ended.append(earlier)
        return ended

    def finish(ended):
        for node in ended:
            while own_pending or len(own_slots) < row_count:
                next_own()
            if node == 0:
                local.wait()
            finish_node(node)

    for node in range(nodes):
        for step in range(1, row_count):
            along_z[node, step].wait_recv()
            deliver(step, node)
            if step == 1 and node + 1 < nodes:
                start_z(node + 1)
                deliver(0, node + 1)
        next_own()
        arrive(node)
        padded(node, weights, chosen)
        if node == 0:
            ancestor_copy.wait()
        if to_core is not None:
            to_core.wait_send()
        given_core[...] = product(node, 1 - core)
        to_core = send(
            given_core, core_in.at[node], core_send.at[node], core_recv.at[node],
            row, col + 1 - 2 * core,
        )
        kept = product(node, core)
        for way in range(2):
            part = kept[:, :, way * half_width:(way + 1) * half_width]
            held[way][0][node] = part.reshape(view(way, mates) + part.shape[1:])
        ended = turn_sums(node)
        to_core.wait_recv()
        for way in range(2):
            part = core_in[node, :, :, halves[way]]
            held[way][0][node] += part.reshape(view(way, mates) + part.shape[1:])
            start_sum(node, way, 0)
        finish(ended)
    for turn in range(nodes, nodes + len(levels)):
        finish(turn_sums(turn))
        for part in range(parts):
            advance(part)
    to_core.wait_send()
    if merged:
        ended = 0
        diag_copy.wait()
        while ended < nodes:
            for part in range(parts):
                advance(part)
            while ended < nodes and all(
                at_step[part] == 2 * steps for part in range(first_of[ended] + (2 if ended else 1))
            ):
                last_steps(ended)
                ended += 1
    for target, remote in delivered:

        @pl.when(target != col)
        def _():
            remote.wait_send()

    for copy in waiting:
        copy.wait_send()


def marks(slot_tiles, blocks, tiles_per_block):
    nodes, slots = slot_tiles.shape
    count = slots // CAP
    shape = (len(blocks), nodes, CAP, tiles_per_block, LANES, count)
    wanted = jnp.stack(blocks).astype(jnp.int32)[:, None, None, None, None, None]
    block = lax.broadcasted_iota(jnp.int32, shape, 5)
    tile = block * tiles_per_block + lax.broadcasted_iota(jnp.int32, shape, 3)
    ids = slot_tiles.reshape(nodes, count, CAP).transpose(0, 2, 1)[None, :, :, None, None, :]
    hits = (ids == tile) & (block == wanted)
    chosen = jnp.sum(jnp.where(hits, 1.0, 0.0).astype(jnp.float32), axis=5)
    return chosen.reshape(len(blocks), nodes, CAP * tiles_per_block, LANES)


def run_kernel(
    merged, ancestor, factor_slots, slot_tiles, parent_factor, diag_inverse, row_count, col_count
):
    nodes, rows, width = factor_slots.shape
    block_rows, block_cols = ancestor.shape
    tiles_per_block = block_cols // TILE
    row, col = lax.axis_index("row"), lax.axis_index("col")
    own_block = row * (col_count // row_count) + col // row_count
    mates, panel_rows = col_count // 2, block_rows // col_count
    gathered = (nodes, row_count * rows, width)
    dma = pltpu.SemaphoreType.DMA
    levels = len(bits_of(col_count)) - 1
    vmem, f32, half_width = pltpu.VMEM, jnp.float32, width // 2
    tail = (panel_rows, half_width)
    low = [vmem((nodes, (mates >> j) // 2, 2) + tail, f32) for j in range(levels)]
    high = [vmem((nodes, 2, (mates >> j) // 2) + tail, f32) for j in range(levels)]
    came = [vmem((nodes, (mates >> j) // 2) + tail, f32) for j in range(levels)]
    parts, steps = 2 * nodes - 1, len(bits_of(row_count)) + len(bits_of(col_count))
    sums = (parts, width * width // LANES, LANES)
    out_shape = [jax.ShapeDtypeStruct((nodes, panel_rows, width), factor_slots.dtype)]
    extra = []
    if merged:
        out_shape += [
            jax.ShapeDtypeStruct((nodes, width, width), f32),
            jax.ShapeDtypeStruct((nodes - 1, width, width), f32),
        ]
        extra = [vmem(sums, f32)] * 3 + [dma((parts, steps))] * 4
    else:
        out_shape += [jax.ShapeDtypeStruct(sums, f32)]
    return pl.pallas_call(
        functools.partial(whole_kernel, row_count, col_count, merged),
        out_shape=out_shape,
        in_specs=[VMEM, ANY, VMEM, VMEM, ANY],
        out_specs=[VMEM] * len(out_shape),
        scratch_shapes=extra + [
            vmem((mates, 2, panel_rows, block_cols), ancestor.dtype),
            dma,
            dma,
            vmem(gathered, factor_slots.dtype),
            vmem((nodes, panel_rows, width), f32),
            vmem(gathered, factor_slots.dtype),
            vmem((nodes, block_cols, width), factor_slots.dtype),
            vmem((row_count - 1, nodes, rows, width), factor_slots.dtype),
            vmem((mates, panel_rows, width), f32),
            vmem((nodes, mates, panel_rows, width), f32),
            dma((row_count - 1, nodes)),
            dma((row_count - 1, nodes)),
            dma((row_count, nodes)),
            dma((row_count, nodes)),
            dma((row_count - 1,)),
            dma((row_count - 1,)),
            dma,
            dma((nodes,)),
            dma((nodes,)),
            dma((nodes, 2, levels)),
            dma((nodes, 2, levels)),
        ] + low + high + came + came,
        compiler_params=pltpu.CompilerParams(
            collective_id=0, has_side_effects=True, vmem_limit_bytes=61 * 2**20
        ),
        name="selected_inverse",
    )(
        marks(slot_tiles, (col, own_block), tiles_per_block),
        ancestor.reshape(mates, 2, panel_rows, block_cols),
        factor_slots, parent_factor, diag_inverse,
    )


def sum_kernel(orders, bounds, given, out, total, landed, rs_send, rs_recv, ag_send, ag_recv):
    index = {"row": lax.axis_index("row"), "col": lax.axis_index("col")}

    def partner(bit):
        axis, weight = bit
        mine = lax.rem(lax.div(index[axis], weight), 2)
        moved = dict(index)
        moved[axis] = index[axis] + (1 - 2 * mine) * weight
        return mine, moved["row"], moved["col"]

    greet([partner(bit)[1:] for bit in sorted(orders[0])])
    steps = len(orders[0])
    starts = [[base] for base, _ in bounds]
    copies = {}
    landing = [base for base, _ in bounds]

    def rows_at(start, length):
        return pl.ds(pl.multiple_of(start, 8), length)

    def halve(part, step):
        half = bounds[part][1] >> (step + 1)
        mine, row, col = partner(orders[part][step])
        start = starts[part][step]
        source = given if step == 0 else total
        copies[part, step] = send(
            source.at[rows_at(start + (1 - mine) * half, half)],
            landed.at[pl.ds(landing[part], half)],
            rs_send.at[part, step], rs_recv.at[part, step], row, col,
        )
        starts[part].append(start + mine * half)

    def add(part, step):
        half = bounds[part][1] >> (step + 1)
        start = starts[part][step + 1]
        source = given if step == 0 else total
        target = out if step == steps - 1 else total
        chunk = min(half, 32)

        def body(turn, carry):
            rows = rows_at(start + turn * chunk, chunk)
            target[rows, :] = (
                source[rows, :] + landed[rows_at(landing[part] + turn * chunk, chunk), :]
            )
            return carry

        lax.fori_loop(0, half // chunk, body, 0)
        landing[part] += half

    def double(part, step):
        length = bounds[part][1] >> (step + 1)
        _, row, col = partner(orders[part][step])
        where = rows_at(starts[part][step + 1], length)
        copies[part, steps + step] = send(
            out.at[where], out.at[where], ag_send.at[part, step], ag_recv.at[part, step], row, col
        )

    parts = range(len(orders))
    for part in parts:
        halve(part, 0)
    for step in range(steps):
        for part in parts:
            copies[part, step].wait_recv()
            add(part, step)
            if step + 1 < steps:
                halve(part, step + 1)
            else:
                double(part, step)
    for step in range(steps - 1, -1, -1):
        for part in parts:
            half = bounds[part][1] >> (step + 1)
            mine, row, col = partner(orders[part][step])
            pltpu.make_async_remote_copy(
                src_ref=out.at[rows_at(starts[part][step + 1], half)],
                dst_ref=out.at[rows_at(starts[part][step] + (1 - mine) * half, half)],
                send_sem=ag_send.at[part, step],
                recv_sem=ag_recv.at[part, step],
                device_id=(row, col),
                device_id_type=pl.DeviceIdType.MESH,
            ).wait_recv()
            if step > 0:
                double(part, step - 1)
    for copy in copies.values():
        copy.wait_send()


def sum_all(given, row_count, col_count):
    rows, width = given.shape
    col_bits, row_bits = bits_of(col_count), bits_of(row_count)
    half = 1 + (len(col_bits) - 1) // 2
    core = [("col", bit) for bit in col_bits[:1]]
    x = [("col", bit) for bit in col_bits[1:half]]
    y = [("col", bit) for bit in col_bits[half:]]
    z = [("row", bit) for bit in row_bits]
    orders = (core + x + y + z, core + y + x + z, core + z + x + y)
    unit = 8 * row_count * col_count
    units = max(3, -(-rows // unit))
    shares = (-(-units * 2 // 5), -(-units * 2 // 5))
    if units < 5:
        shares = (1, 1)
    shares = shares + (units - sum(shares),)
    bounds, base = [], 0
    for share in shares:
        bounds.append((base, share * unit))
        base += share * unit
    if base > rows:
        given = jnp.concatenate([given, jnp.zeros((base - rows, width), given.dtype)])
    shape = (base, width)
    dma = pltpu.SemaphoreType.DMA((len(orders), len(orders[0])))
    out = pl.pallas_call(
        functools.partial(sum_kernel, orders, bounds),
        out_shape=jax.ShapeDtypeStruct(shape, given.dtype),
        in_specs=[VMEM],
        out_specs=VMEM,
        scratch_shapes=[
            pltpu.VMEM(shape, given.dtype),
            pltpu.VMEM(shape, given.dtype),
            dma, dma, dma, dma,
        ],
        compiler_params=pltpu.CompilerParams(
            collective_id=1, has_side_effects=True, vmem_limit_bytes=56 * 2**20
        ),
        name="sum_all",
    )(given)
    return out[:rows]


def on_device(ancestor_inverse, factor_slots, slot_tiles, parent_factor, diag_inverse):
    row_count = lax.axis_size("row")
    col_count = lax.axis_size("col")
    nodes, _, width = factor_slots.shape
    merged = ancestor_inverse.shape[0] * width <= MERGED_SIZE
    results = run_kernel(
        merged, ancestor_inverse, factor_slots, slot_tiles, parent_factor, diag_inverse,
        row_count, col_count,
    )
    if merged:
        return tuple(results)
    panels, sums = results
    sums = sums.reshape(2 * nodes - 1, -1, width, LANES).transpose(0, 2, 1, 3)
    totals = sum_all(sums.reshape(-1, width), row_count, col_count)
    totals = totals.reshape(-1, width, width)
    diagonals = [diag_inverse[0] - totals[0]]
    parents = []
    for node in range(1, nodes):
        link = parent_factor[node - 1].astype(jnp.float32)
        upper = -(
            totals[2 * node] + jnp.dot(diagonals[-1], link, precision=exact_mode)
        )
        parents.append(upper)
        diagonals.append(
            diag_inverse[node] - totals[2 * node - 1]
            - jnp.dot(link.T, upper, precision=exact_mode)
        )
    return panels, jnp.stack(diagonals), jnp.stack(parents)


def solution(mesh):
    placed = (P("row", "col"), P(None, ("row", "col"), None), P(), P(), P())
    return jax.shard_map(
        on_device,
        mesh=mesh,
        in_specs=placed,
        out_specs=(P(None, ("row", "col"), None), P(), P()),
        check_vma=False,
    )
```
